256 devices in a mesh: layer: 8 (over y, core), sensor: 8 (over z), row: 4 (over x).
Axes of the slice: x: 4, y: 4, z: 8, core: 2. Of those that a mesh axis runs over, the one named last changes fastest.
Arguments:
- layers_init: float32 [4, 2048, 2048], P(None, ('layer', 'row')), may hold values from -6 to 6
- residual_init: float32 [8, 4096, 128], P('sensor', ('layer', 'row')), may hold values from -6 to 6
- foot_shift: int32 [8, 4], P('sensor'), may hold values from 0 to 3071, as said below
- blocks: float32 [8, 4, 4, 128, 128], P('sensor'), may hold values from -0.25 to 0.25
- precond: float32 [4, 128, 128], replicated
- omega: float32 [4], replicated, may hold values from 0.1 to 0.25
- beta: float32 [4], replicated, may hold values from 0.02 to 0.1
Outputs:
- layers_out: float32 [4, 2048, 2048], P(None, ('layer', 'row'))
- residual_out: float32 [8, 4096, 128], P('sensor', ('layer', 'row'))
The draws below stay inside these ranges and needn't reach their ends.
Inputs may be any that keep to these rules, and one draw needn't show every extreme that they name: `foot_shift`: zero on layer 0 for every sensor; sensor 0 on the last layer has the largest value.
All inputs are finite; a program needn't handle non-finite values.
Results may differ from the reference program's by a relative error of at most 0.0003.
Values sent between devices are 32-bit elements; how exact they have to be, the bound alone decides.
A program may use at most 64 MiB of HBM per device.

```python
import math
import jax
import jax.numpy as jnp
from jax import lax

NG = 2048
TILE = 128
K = 4
NOFF = 3
LAYERS = 4
SWEEPS = 3
NS = 8
NST = 4096
NTL = 32768
TPD = 1024
TD = 128


def draw_foot_shift(key, part):
    key_shift = jax.random.fold_in(key, 21)
    shifts = jax.random.randint(key_shift, (NS, LAYERS), 0, NOFF * TPD, jnp.int32)
    shifts = shifts.at[:, 0].set(0)
    shifts = shifts.at[0, LAYERS - 1].set(NOFF * TPD - 1)
    return shifts.astype(jnp.int32)


def draw_precond(key, part):
    key_off = jax.random.fold_in(key, 11)
    key_diag = jax.random.fold_in(key, 12)
    spread = 0.03
    diag_vals = jax.random.uniform(key_diag, (LAYERS, TILE), jnp.float32, 0.8, 1.2)
    upper = jax.random.uniform(key_off, (LAYERS, TILE, TILE), jnp.float32, -spread, spread)
    sym = upper + jnp.swapaxes(upper, 1, 2)
    ident = (jnp.arange(TILE)[:, None] == jnp.arange(TILE)[None, :]).astype(jnp.float32)
    return sym * (1.0 - ident)[None] + ident[None] * diag_vals[:, :, None]


def block_scale(rng, extent, pieces, least, high):
    gain, own = 1.0, jax.random.fold_in(rng, 6)
    for dim, parts in pieces:
        steps = jnp.exp(jax.random.uniform(jax.random.fold_in(own, dim), (parts,), jnp.float32, least / len(pieces), high / len(pieces)))
        gain = gain * jnp.repeat(steps, extent[dim] // parts).reshape([-1 if axis == dim else 1 for axis in range(len(extent))])
    return gain


def gaussian(key, shape, width, most, split=(), kind=jnp.bfloat16):
    gain = block_scale(key, shape, split, -0.22, 0.18) if split else 1.0
    values = jax.random.normal(key, shape, jnp.float32) * width * gain
    return jnp.minimum(jnp.maximum(values, -most), most).astype(kind)


def setup_inputs(seed: int = 0) -> dict:
    splits = jax.random.split(jax.random.key(seed), 8)
    return {
        "layers_init": gaussian(splits[0], (LAYERS, NG, NG), 1.0, 6.0, ((1, 32),), jnp.float32),
        "residual_init": gaussian(splits[1], (NS, NST, TILE), 1.0, 6.0, ((0, 8), (1, 32)), jnp.float32),
        "foot_shift": draw_foot_shift(jax.random.fold_in(splits[7], 71), 0),
        "blocks": gaussian(splits[3], (NS, LAYERS, K, TILE, TILE), (TILE * K) ** -0.5, 0.25, ((0, 8),), jnp.float32),
        "precond": draw_precond(jax.random.fold_in(splits[7], 71), 0),
        "omega": jnp.clip(jax.random.uniform(splits[5], (LAYERS,), jnp.float32, 0.1, 0.25), 0.1, 0.25),
        "beta": jnp.clip(jnp.exp(jax.random.uniform(splits[6], (LAYERS,), jnp.float32, math.log(0.02), math.log(0.1))), 0.02, 0.1),
    }


def laplace_of(field):
    padded = jnp.pad(field, 1)
    return 4.0 * field - padded[2:, 1:-1] - padded[:-2, 1:-1] - padded[1:-1, 2:] - padded[1:-1, :-2]


def reference(layers_init, residual_init, foot_shift, blocks, precond, omega, beta):
    highest = lax.Precision.HIGHEST
    tile_rows = jnp.arange(NST, dtype=jnp.int32)
    entries = jnp.arange(K, dtype=jnp.int32)
    local_pos = (((tile_rows[:, None] % TD) * K + entries[None, :]) * TPD) // (TD * K)
    base_tile = (tile_rows[:, None] // TD) * TPD + local_pos
    foot_tile = (base_tile[None, None] + foot_shift[:, :, None, None]).astype(jnp.int32)
    fields = layers_init
    residual = residual_init
    for sweep_index in range(SWEEPS):
        for layer in range(LAYERS):
            def back_one(total, inputs):
                sensor_rows, sensor_blocks, sensor_tiles = inputs
                products = jnp.einsum("jc,kdc->jkd", sensor_rows, sensor_blocks, precision=highest)
                return total.at[sensor_tiles.reshape(-1)].add(products.reshape(-1, TILE), mode="drop"), None

            back, _ = lax.scan(back_one, jnp.zeros((NTL, TILE), jnp.float32),
                               (residual, blocks[:, layer], foot_tile[:, layer]))
            field = fields[layer]
            laplace = laplace_of(field).reshape(NTL, TILE)
            update = omega[layer] * jnp.dot(back - beta[layer] * laplace, precond[layer], precision=highest)
            fields = fields.at[layer].set(field + update.reshape(NG, NG))
            update_padded = jnp.concatenate([update, jnp.zeros((1, TILE), jnp.float32)], axis=0)

            def forward_one(state_none, inputs):
                sensor_rows, sensor_blocks, sensor_tiles = inputs
                selected = update_padded[jnp.minimum(sensor_tiles, NTL).astype(jnp.int32)]
                change = jnp.einsum("jkc,kcd->jd", selected, sensor_blocks, precision=highest)
                return state_none, sensor_rows - change

            _, residual = lax.scan(forward_one, jnp.zeros((), jnp.float32),
                                   (residual, blocks[:, layer], foot_tile[:, layer]))
    return fields, residual
```

```python
import functools

import jax
import jax.numpy as jnp
from jax import lax
from jax.experimental import pallas as pl
from jax.experimental.pallas import tpu as pltpu
from jax.sharding import PartitionSpec as P

MESH = pl.DeviceIdType.MESH
SWEEPS = 3
LAYERS = 4
NS = 8
NB = 32
ROWB = 4
TD = 128
TILE = 128
PIECE = 64
WIN = 144
LEAD = 16
REACH = 3
ORDER = (4, 3, 5, 2, 6, 1, 7)
FROM = ((-3, -2, -1), (-3, -2, -1, 1, 2, 3), (-3, -2, -1, 1, 2, 3), (1, 2, 3))
SLOT0 = (0, 3, 9, 15)


def split(x):
    hi = x.astype(jnp.bfloat16)
    return hi, (x - hi.astype(jnp.float32)).astype(jnp.bfloat16)


def dot3(x, w_hi, w_lo):
    hi, lo = split(x)
    dot = functools.partial(jnp.dot, preferred_element_type=jnp.float32)
    return dot(hi, w_hi) + (dot(lo, w_hi) + dot(hi, w_lo))


def kernel(shift, omega, beta, layers_in, residual_in, wt_hi, wt_lo, w_hi, w_lo, m_hi, m_lo,
           layers_out, residual_out,
           field, win, frame, slots, flat, b_send, b_recv, c_send, halves, par_send, par,
           acc, upd, halo_send, halo_recv,
           local_sem, slot_ssem, slot_rsem, b_ssem, b_rsem, c_ssem, c_rsem, p_ssem, p_rsem,
           h_ssem, h_rsem, f_ssem, f_rsem):
    lay, me, row = lax.axis_index("layer"), lax.axis_index("sensor"), lax.axis_index("row")
    block = lay * ROWB + row

    def at_block(dist):
        other = lax.rem(block + (dist + NB), NB)
        return (other // ROWB, me, lax.rem(other, ROWB))

    def at_sensor(dist):
        return (lay, lax.rem(me + dist, NS), row)

    first, last = me == 0, me == NS - 1
    up_block = lax.rem(block + NB - first.astype(jnp.int32), NB)
    down_block = lax.rem(block + last.astype(jnp.int32), NB)
    above = (up_block // ROWB, lax.rem(me + NS - 1, NS), lax.rem(up_block, ROWB))
    below = (down_block // ROWB, lax.rem(me + 1, NS), lax.rem(down_block, ROWB))

    barrier = pltpu.get_barrier_semaphore()
    partners = [at_sensor(d) for d in range(1, NS)]
    partners += [at_block(d) for d in (-3, -2, -1, 1, 2, 3)] + [above, below]
    load = pltpu.make_async_copy(layers_in.at[:, pl.ds(pl.multiple_of(me * 8, 8), 8), :], field, local_sem)
    load.start()
    frame[...] = jnp.zeros_like(frame)
    halves[...] = jnp.zeros_like(halves)
    win[pl.ds(0, LEAD), :] = jnp.zeros((LEAD, TILE), jnp.float32)
    win[pl.ds(LEAD, TD), :] = residual_in[0]
    odd = [lax.rem(shift[0, l], 2) for l in range(LAYERS)]
    half = [lax.rem(shift[0, l], 8) // 2 for l in range(LAYERS)]
    lag = [shift[0, l] // 8 for l in range(LAYERS)]
    for l in range(LAYERS):
        par_send[pl.ds(l, 1), :] = jnp.full((1, TILE), odd[l].astype(jnp.float32))
    par_send[pl.ds(LAYERS, 8 - LAYERS), :] = jnp.zeros((8 - LAYERS, TILE), jnp.float32)
    par[me] = par_send[...]
    load.wait()
    for other in partners:
        pl.semaphore_signal(barrier, inc=1, device_id=other, device_id_type=MESH)
    pl.semaphore_wait(barrier, len(partners))

    def par_copy(d):
        return pltpu.make_async_remote_copy(
            par_send, par.at[me], p_ssem.at[d], p_rsem.at[d], device_id=at_sensor(d), device_id_type=MESH)

    def halo_copies(l, slot):
        return [
            pltpu.make_async_remote_copy(
                halo_send.at[l, 0], halo_recv.at[slot, l, 1], h_ssem.at[l, 0], h_rsem.at[slot, l, 1],
                device_id=above, device_id_type=MESH),
            pltpu.make_async_remote_copy(
                halo_send.at[l, 1], halo_recv.at[slot, l, 0], h_ssem.at[l, 1], h_rsem.at[slot, l, 0],
                device_id=below, device_id_type=MESH),
        ]

    def halo_start(l, slot):
        halo_send[l, 0] = field[l, pl.ds(0, 1), :]
        halo_send[l, 1] = field[l, pl.ds(7, 1), :]
        for copy in halo_copies(l, slot):
            copy.start()

    for d in ORDER:
        par_copy(d).start()
    for l in range(LAYERS):
        halo_start(l, 0)

    def b_copy(d):
        return pltpu.make_async_remote_copy(
            b_send.at[d], b_recv.at[d], b_ssem.at[d], b_rsem.at[d], device_id=at_sensor(d), device_id_type=MESH)

    def c_copy(d):
        return pltpu.make_async_remote_copy(
            c_send.at[d], halves.at[pl.ds(pl.multiple_of(64 + PIECE * me, 8), PIECE), :], c_ssem.at[d], c_rsem.at[d],
            device_id=at_sensor(d), device_id_type=MESH)

    def f_copy(l, d):
        return pltpu.make_async_remote_copy(
            field.at[l], layers_out.at[l, pl.ds(pl.multiple_of(me * 8, 8), 8), :], f_ssem.at[l, d], f_rsem.at[l, d],
            device_id=at_sensor(d), device_id_type=MESH)

    def slot_copy(l, n, dist):
        return pltpu.make_async_remote_copy(
            win.at[pl.ds(8, WIN - 8), :], slots.at[SLOT0[l] + n], slot_ssem.at[SLOT0[l] + n], slot_rsem.at[SLOT0[l] + n],
            device_id=at_block(-dist), device_id_type=MESH)

    index = lax.broadcasted_iota(jnp.int32, (WIN, TILE), 0)
    cell_row = lax.broadcasted_iota(jnp.int32, (8, 2048), 0)
    cell_col = lax.broadcasted_iota(jnp.int32, (8, 2048), 1)
    at_top = jnp.logical_and(block == 0, first)
    at_bottom = jnp.logical_and(block == NB - 1, last)

    def step(sweep, l):
        inside = index >= LEAD + lag[l] - TD * block
        products = dot3(jnp.where(inside, win[...], 0.0), wt_hi[l], wt_lo[l])
        for k in range(4):
            flat[pl.ds(k, WIN, stride=4), :] = products[:, k * TILE:(k + 1) * TILE]
        for d in ORDER:
            to = lax.rem(me + d, NS)
            b_send[d] = flat[pl.ds(64 + PIECE * to - half[l], PIECE), :]
            b_copy(d).start()
        own = flat[pl.ds(64 + PIECE * me - half[l], PIECE), :]
        slot = lax.rem(sweep, 2)
        for copy in halo_copies(l, slot):
            copy.wait_recv()
        f = field[l]
        top = jnp.where(at_top, 0.0, halo_recv[slot, l, 0])
        bottom = jnp.where(at_bottom, 0.0, halo_recv[slot, l, 1])
        north = jnp.where(cell_row == 0, top, pltpu.roll(f, 1, 0))
        south = jnp.where(cell_row == 7, bottom, pltpu.roll(f, 7, 0))
        west = jnp.where(cell_col == 0, 0.0, pltpu.roll(f, 1, 1))
        east = jnp.where(cell_col == 2047, 0.0, pltpu.roll(f, 2047, 1))
        laplace = 4.0 * f - north - south - west - east

        if l == 0:
            @pl.when(sweep == 0)
            def _():
                for d in ORDER:
                    par_copy(d).wait_recv()

        is_odd = par[me, pl.ds(l, 1), :] > 0.5
        even_sum = jnp.where(is_odd, 0.0, own)
        odd_sum = jnp.where(is_odd, own, 0.0)
        for d in reversed(ORDER):
            b_copy(d).wait_recv()
            other = lax.rem(me + (NS - d), NS)
            piece = b_recv[d]
            is_odd = par[other, pl.ds(l, 1), :] > 0.5
            even_sum = even_sum + jnp.where(is_odd, 0.0, piece)
            odd_sum = odd_sum + jnp.where(is_odd, piece, 0.0)
        acc[0] = even_sum
        acc[1] = odd_sum
        weight = beta[l]
        gradient = jnp.concatenate(
            [
                acc[c % 2, pl.ds(c // 2, 8, stride=8), :] - weight * laplace[:, c * TILE:(c + 1) * TILE]
                for c in range(16)
            ], axis=0)
        update = omega[l] * dot3(gradient, m_hi[l], m_lo[l])
        for c in range(16):
            upd[c % 2, pl.ds(c // 2, 8, stride=8), :] = update[8 * c:8 * c + 8]
        for d in ORDER:
            other = lax.rem(me + d, NS)
            c_send[d] = jnp.where(par[other, pl.ds(l, 1), :] > 0.5, upd[1], upd[0])
            c_copy(d).start()
        halves[pl.ds(pl.multiple_of(64 + PIECE * me, 8), PIECE), :] = jnp.where(
            par[me, pl.ds(l, 1), :] > 0.5, upd[1], upd[0])
        for c in range(16):
            field[l, :, c * TILE:(c + 1) * TILE] = f[:, c * TILE:(c + 1) * TILE] + update[8 * c:8 * c + 8]
        for copy in halo_copies(l, slot):
            copy.wait_send()

        @pl.when(sweep < SWEEPS - 1)
        def _():
            halo_start(l, 1 - slot)

        @pl.when(sweep == SWEEPS - 1)
        def _():
            for d in ORDER:
                f_copy(l, d).start()

        for d in ORDER:
            b_copy(d).wait_send()
        for d in ORDER:
            c_copy(d).wait_recv()
        chosen = jnp.concatenate(
            [halves[pl.ds(half[l] + k, WIN, stride=4), :] for k in range(4)], axis=1)
        change = dot3(chosen, w_hi[l], w_lo[l])
        win[...] = jnp.where(index == LEAD - 1, 0.0, win[...]) - jnp.where(inside, change, 0.0)
        for d in ORDER:
            c_copy(d).wait_send()

    def reframe(l):
        sources = FROM[l]
        for n, dist in enumerate(sources):
            slot_copy(l, n, dist).start()
        least = min(sources[0], 0)
        base = -least * TD
        frame[pl.ds(LEAD + base, TD), :] = win[pl.ds(LEAD, TD), :]
        for n, dist in enumerate(sources):
            slot_copy(l, n, dist).wait_recv()
        for n, dist in enumerate(sources):
            frame[pl.ds(LEAD + base + dist * TD, TD), :] = slots[SLOT0[l] + n, pl.ds(8, TD), :]
        for n, dist in enumerate(sources):
            if dist > least:
                at = pl.ds(LEAD - 1 + base + dist * TD, 1)
                frame[at, :] = frame[at, :] + slots[SLOT0[l] + n, pl.ds(7, 1), :]
        if least < 0:
            at = pl.ds(LEAD - 1 + base, 1)
            frame[at, :] = frame[at, :] + win[pl.ds(LEAD - 1, 1), :]
        moved = frame[pl.ds(base + lag[l] - lag[(l + 1) % LAYERS], WIN), :]
        for n, dist in enumerate(sources):
            slot_copy(l, n, dist).wait_send()
        win[...] = moved

    def turn(sweep, carry):
        for l in range(LAYERS):
            step(sweep, l)
            reframe(l)
        return carry

    lax.fori_loop(0, SWEEPS, turn, 0)
    residual_out[0] = win[pl.ds(LEAD, TD), :]
    store = pltpu.make_async_copy(field, layers_out.at[:, pl.ds(pl.multiple_of(me * 8, 8), 8), :], local_sem)
    store.start()
    for d in ORDER:
        par_copy(d).wait_send()
    for l in range(LAYERS):
        for d in ORDER:
            f_copy(l, d).wait()
    store.wait()


def halves_of(x):
    hi = lax.reduce_precision(x, exponent_bits=8, mantissa_bits=7)
    return hi.astype(jnp.bfloat16), (x - hi).astype(jnp.bfloat16)


def per_device(layers_init, residual_init, foot_shift, blocks, precond, omega, beta):
    w = blocks[0]
    w_hi, w_lo = halves_of(w.reshape(LAYERS, 4 * TILE, TILE))
    wt_hi, wt_lo = halves_of(jnp.transpose(w, (0, 3, 1, 2)).reshape(LAYERS, TILE, 4 * TILE))
    m_hi, m_lo = halves_of(precond)
    smem = pl.BlockSpec(memory_space=pltpu.SMEM)
    vmem = pl.BlockSpec(memory_space=pltpu.VMEM)
    hbm = pl.BlockSpec(memory_space=pl.ANY)
    f32 = jnp.float32
    dma = pltpu.SemaphoreType.DMA
    return pl.pallas_call(
        kernel,
        out_shape=(
            jax.ShapeDtypeStruct(layers_init.shape, f32),
            jax.ShapeDtypeStruct(residual_init.shape, f32),
        ),
        in_specs=[smem, smem, smem, hbm] + [vmem] * 7,
        out_specs=(hbm, vmem),
        scratch_shapes=[
            pltpu.VMEM((LAYERS, 8, 2048), f32),
            pltpu.VMEM((WIN, TILE), f32),
            pltpu.VMEM((LEAD + 7 * TD, TILE), f32),
            pltpu.VMEM((18, WIN - 8, TILE), f32),
            pltpu.VMEM((4 * WIN, TILE), f32),
            pltpu.VMEM((NS, PIECE, TILE), f32),
            pltpu.VMEM((NS, PIECE, TILE), f32),
            pltpu.VMEM((NS, PIECE, TILE), f32),
            pltpu.VMEM((4 * WIN + 8, TILE), f32),
            pltpu.VMEM((8, TILE), f32),
            pltpu.VMEM((NS, 8, TILE), f32),
            pltpu.VMEM((2, PIECE, TILE), f32),
            pltpu.VMEM((2, PIECE, TILE), f32),
            pltpu.VMEM((LAYERS, 2, 1, 2048), f32),
            pltpu.VMEM((2, LAYERS, 2, 1, 2048), f32),
            dma, dma((18,)), dma((18,)), dma((NS,)), dma((NS,)), dma((NS,)), dma((NS,)), dma((NS,)), dma((NS,)),
            dma((LAYERS, 2)), dma((2, LAYERS, 2)), dma((LAYERS, NS)), dma((LAYERS, NS)),
        ],
        compiler_params=pltpu.CompilerParams(
            collective_id=0, has_side_effects=True, vmem_limit_bytes=40 * 2**20
        ),
    )(foot_shift, omega, beta, layers_init, residual_init, wt_hi, wt_lo, w_hi, w_lo, m_hi, m_lo)


def solution(mesh):
    in_specs = (
        P(None, ("layer", "row"), None),
        P("sensor", ("layer", "row"), None),
        P("sensor", None),
        P("sensor", None, None, None, None),
        P(),
        P(),
        P(),
    )
    out_specs = (P(None, ("layer", "row"), None), P("sensor", ("layer", "row"), None))
    return jax.shard_map(
        per_device, mesh=mesh, in_specs=in_specs, out_specs=out_specs, check_vma=False
    )
```

```python
import functools

import jax
import jax.numpy as jnp
from jax import lax
from jax.experimental import pallas as pl
from jax.experimental.pallas import tpu as pltpu
from jax.sharding import PartitionSpec as P

MESH = pl.DeviceIdType.MESH
SWEEPS = 3
LAYERS = 4
NS = 8
NB = 32
ROWB = 4
TD = 128
TILE = 128
PIECE = 64
PARTS = 2
PART = PIECE // PARTS
WIN = 144
LEAD = 16
REACH = 3
ORDER = (4, 3, 5, 2, 6, 1, 7)
FROM = ((-3, -2, -1), (-3, -2, -1, 1, 2, 3), (-3, -2, -1, 1, 2, 3), (1, 2, 3))
SLOT0 = (0, 3, 9, 15)


def split(x):
    hi = x.astype(jnp.bfloat16)
    return hi, (x - hi.astype(jnp.float32)).astype(jnp.bfloat16)


def dot3(x, w_hi, w_lo):
    hi, lo = split(x)
    dot = functools.partial(jnp.dot, preferred_element_type=jnp.float32)
    return dot(hi, w_hi) + (dot(lo, w_hi) + dot(hi, w_lo))


def kernel(shift, omega, beta, layers_in, residual_in, wt_hi, wt_lo, w_hi, w_lo, m_hi, m_lo,
           layers_out, residual_out,
           field, win, frame, slots, flat, b_send, b_recv, c_send, halves, par_send, par,
           lap, upd, halo_send, halo_recv,
           local_sem, slot_ssem, slot_rsem, b_ssem, b_rsem, c_ssem, c_rsem, p_ssem, p_rsem,
           h_ssem, h_rsem, f_ssem, f_rsem):
    lay, me, row = lax.axis_index("layer"), lax.axis_index("sensor"), lax.axis_index("row")
    block = lay * ROWB + row

    def at_block(dist):
        other = lax.rem(block + (dist + NB), NB)
        return (other // ROWB, me, lax.rem(other, ROWB))

    def at_sensor(dist):
        return (lay, lax.rem(me + dist, NS), row)

    first, last = me == 0, me == NS - 1
    up_block = lax.rem(block + NB - first.astype(jnp.int32), NB)
    down_block = lax.rem(block + last.astype(jnp.int32), NB)
    above = (up_block // ROWB, lax.rem(me + NS - 1, NS), lax.rem(up_block, ROWB))
    below = (down_block // ROWB, lax.rem(me + 1, NS), lax.rem(down_block, ROWB))

    barrier = pltpu.get_barrier_semaphore()
    partners = [at_sensor(d) for d in range(1, NS)]
    partners += [at_block(d) for d in (-3, -2, -1, 1, 2, 3)] + [above, below]
    load = pltpu.make_async_copy(layers_in.at[:, pl.ds(pl.multiple_of(me * 8, 8), 8), :], field, local_sem)
    load.start()
    frame[...] = jnp.zeros_like(frame)
    halves[...] = jnp.zeros_like(halves)
    win[pl.ds(0, LEAD), :] = jnp.zeros((LEAD, TILE), jnp.float32)
    win[pl.ds(LEAD, TD), :] = residual_in[0]
    odd = [lax.rem(shift[0, l], 2) for l in range(LAYERS)]
    half = [lax.rem(shift[0, l], 8) // 2 for l in range(LAYERS)]
    lag = [shift[0, l] // 8 for l in range(LAYERS)]
    for l in range(LAYERS):
        par_send[pl.ds(l, 1), :] = jnp.full((1, TILE), odd[l].astype(jnp.float32))
    par_send[pl.ds(LAYERS, 8 - LAYERS), :] = jnp.zeros((8 - LAYERS, TILE), jnp.float32)
    par[me] = par_send[...]
    load.wait()
    for other in partners:
        pl.semaphore_signal(barrier, inc=1, device_id=other, device_id_type=MESH)
    pl.semaphore_wait(barrier, len(partners))

    def par_copy(d):
        return pltpu.make_async_remote_copy(
            par_send, par.at[me], p_ssem.at[d], p_rsem.at[d], device_id=at_sensor(d), device_id_type=MESH)

    def halo_copies(l, slot):
        return [
            pltpu.make_async_remote_copy(
                halo_send.at[l, 0], halo_recv.at[slot, l, 1], h_ssem.at[l, 0], h_rsem.at[slot, l, 1],
                device_id=above, device_id_type=MESH),
            pltpu.make_async_remote_copy(
                halo_send.at[l, 1], halo_recv.at[slot, l, 0], h_ssem.at[l, 1], h_rsem.at[slot, l, 0],
                device_id=below, device_id_type=MESH),
        ]

    def halo_start(l, slot):
        halo_send[l, 0] = field[l, pl.ds(0, 1), :]
        halo_send[l, 1] = field[l, pl.ds(7, 1), :]
        for copy in halo_copies(l, slot):
            copy.start()

    for d in ORDER:
        par_copy(d).start()
    for l in range(LAYERS):
        halo_start(l, 0)

    def b_copy(d, q):
        part = pl.ds(PART * q, PART)
        return pltpu.make_async_remote_copy(
            b_send.at[d, part, :], b_recv.at[d, part, :], b_ssem.at[q, d], b_rsem.at[q, d], device_id=at_sensor(d), device_id_type=MESH)

    def own_half(q):
        return pl.ds(pl.multiple_of(64 + PIECE * me + PART * q, 8), PART)

    def c_copy(d, q):
        return pltpu.make_async_remote_copy(
            c_send.at[d, pl.ds(PART * q, PART), :], halves.at[own_half(q), :], c_ssem.at[q, d], c_rsem.at[q, d],
            device_id=at_sensor(d), device_id_type=MESH)

    def f_copy(l, d):
        return pltpu.make_async_remote_copy(
            field.at[l], layers_out.at[l, pl.ds(pl.multiple_of(me * 8, 8), 8), :], f_ssem.at[l, d], f_rsem.at[l, d],
            device_id=at_sensor(d), device_id_type=MESH)

    def slot_copy(l, n, dist):
        return pltpu.make_async_remote_copy(
            win.at[pl.ds(8, WIN - 8), :], slots.at[SLOT0[l] + n], slot_ssem.at[SLOT0[l] + n], slot_rsem.at[SLOT0[l] + n],
            device_id=at_block(-dist), device_id_type=MESH)

    index = lax.broadcasted_iota(jnp.int32, (WIN, TILE), 0)
    cell_row = lax.broadcasted_iota(jnp.int32, (8, 2048), 0)
    cell_col = lax.broadcasted_iota(jnp.int32, (8, 2048), 1)
    at_top = jnp.logical_and(block == 0, first)
    at_bottom = jnp.logical_and(block == NB - 1, last)

    def step(sweep, l):
        inside = index >= LEAD + lag[l] - TD * block
        products = dot3(jnp.where(inside, win[...], 0.0), wt_hi[l], wt_lo[l])
        for k in range(4):
            flat[pl.ds(k, WIN, stride=4), :] = products[:, k * TILE:(k + 1) * TILE]
        for q in range(PARTS):
            for d in ORDER:
                to = lax.rem(me + d, NS)
                b_send[d, pl.ds(PART * q, PART), :] = flat[pl.ds(64 + PIECE * to + PART * q - half[l], PART), :]
                b_copy(d, q).start()
        own = flat[pl.ds(64 + PIECE * me - half[l], PIECE), :]
        slot = lax.rem(sweep, 2)
        for copy in halo_copies(l, slot):
            copy.wait_recv()
        f = field[l]
        top = jnp.where(at_top, 0.0, halo_recv[slot, l, 0])
        bottom = jnp.where(at_bottom, 0.0, halo_recv[slot, l, 1])
        north = jnp.where(cell_row == 0, top, pltpu.roll(f, 1, 0))
        south = jnp.where(cell_row == 7, bottom, pltpu.roll(f, 7, 0))
        west = jnp.where(cell_col == 0, 0.0, pltpu.roll(f, 1, 1))
        east = jnp.where(cell_col == 2047, 0.0, pltpu.roll(f, 2047, 1))
        laplace = 4.0 * f - north - south - west - east

        if l == 0:
            @pl.when(sweep == 0)
            def _():
                for d in ORDER:
                    par_copy(d).wait_recv()

        weight = -beta[l]
        for c in range(16):
            lap[c % 2, pl.ds(c // 2, 8, stride=8), :] = weight * laplace[:, c * TILE:(c + 1) * TILE]
        is_odd = par[me, pl.ds(l, 1), :] > 0.5
        is_odd_from = {d: par[lax.rem(me + (NS - d), NS), pl.ds(l, 1), :] > 0.5 for d in ORDER}
        is_odd_to = {d: is_odd_from[NS - d] for d in ORDER}
        for q in range(PARTS):
            part = pl.ds(PART * q, PART)
            mine = own[PART * q:PART * (q + 1)]
            even_sum = lap[0, part, :] + jnp.where(is_odd, 0.0, mine)
            odd_sum = lap[1, part, :] + jnp.where(is_odd, mine, 0.0)
            for d in reversed(ORDER):
                b_copy(d, q).wait_recv()
                piece = b_recv[d, part, :]
                even_sum = even_sum + jnp.where(is_odd_from[d], 0.0, piece)
                odd_sum = odd_sum + jnp.where(is_odd_from[d], piece, 0.0)
            update = omega[l] * dot3(jnp.concatenate([even_sum, odd_sum], axis=0), m_hi[l], m_lo[l])
            even, odd_ = update[:PART], update[PART:]
            for d in ORDER:
                c_send[d, part, :] = jnp.where(is_odd_to[d], odd_, even)
                c_copy(d, q).start()
            upd[0, part, :] = even
            upd[1, part, :] = odd_
            halves[own_half(q), :] = jnp.where(is_odd, odd_, even)
        for c in range(16):
            field[l, :, c * TILE:(c + 1) * TILE] = (
                f[:, c * TILE:(c + 1) * TILE] + upd[c % 2, pl.ds(c // 2, 8, stride=8), :])
        for copy in halo_copies(l, slot):
            copy.wait_send()

        @pl.when(sweep < SWEEPS - 1)
        def _():
            halo_start(l, 1 - slot)

        @pl.when(sweep == SWEEPS - 1)
        def _():
            for d in ORDER:
                f_copy(l, d).start()

        for q in range(PARTS):
            for d in ORDER:
                b_copy(d, q).wait_send()
        for q in range(PARTS):
            for d in ORDER:
                c_copy(d, q).wait_recv()
        chosen = jnp.concatenate(
            [halves[pl.ds(half[l] + k, WIN, stride=4), :] for k in range(4)], axis=1)
        change = dot3(chosen, w_hi[l], w_lo[l])
        win[...] = jnp.where(index == LEAD - 1, 0.0, win[...]) - jnp.where(inside, change, 0.0)
        for q in range(PARTS):
            for d in ORDER:
                c_copy(d, q).wait_send()

    def reframe(l):
        sources = FROM[l]
        for n, dist in enumerate(sources):
            slot_copy(l, n, dist).start()
        least = min(sources[0], 0)
        base = -least * TD
        frame[pl.ds(LEAD + base, TD), :] = win[pl.ds(LEAD, TD), :]
        for n, dist in enumerate(sources):
            slot_copy(l, n, dist).wait_recv()
        for n, dist in enumerate(sources):
            frame[pl.ds(LEAD + base + dist * TD, TD), :] = slots[SLOT0[l] + n, pl.ds(8, TD), :]
        for n, dist in enumerate(sources):
            if dist > least:
                at = pl.ds(LEAD - 1 + base + dist * TD, 1)
                frame[at, :] = frame[at, :] + slots[SLOT0[l] + n, pl.ds(7, 1), :]
        if least < 0:
            at = pl.ds(LEAD - 1 + base, 1)
            frame[at, :] = frame[at, :] + win[pl.ds(LEAD - 1, 1), :]
        moved = frame[pl.ds(base + lag[l] - lag[(l + 1) % LAYERS], WIN), :]
        for n, dist in enumerate(sources):
            slot_copy(l, n, dist).wait_send()
        win[...] = moved

    def turn(sweep, carry):
        for l in range(LAYERS):
            step(sweep, l)
            reframe(l)
        return carry

    lax.fori_loop(0, SWEEPS, turn, 0)
    residual_out[0] = win[pl.ds(LEAD, TD), :]
    store = pltpu.make_async_copy(field, layers_out.at[:, pl.ds(pl.multiple_of(me * 8, 8), 8), :], local_sem)
    store.start()
    for d in ORDER:
        par_copy(d).wait_send()
    for l in range(LAYERS):
        for d in ORDER:
            f_copy(l, d).wait()
    store.wait()


def halves_of(x):
    hi = lax.reduce_precision(x, exponent_bits=8, mantissa_bits=7)
    return hi.astype(jnp.bfloat16), (x - hi).astype(jnp.bfloat16)


def per_device(layers_init, residual_init, foot_shift, blocks, precond, omega, beta):
    w = blocks[0]
    w_hi, w_lo = halves_of(w.reshape(LAYERS, 4 * TILE, TILE))
    wt_hi, wt_lo = halves_of(jnp.transpose(w, (0, 3, 1, 2)).reshape(LAYERS, TILE, 4 * TILE))
    m_hi, m_lo = halves_of(precond)
    smem = pl.BlockSpec(memory_space=pltpu.SMEM)
    vmem = pl.BlockSpec(memory_space=pltpu.VMEM)
    hbm = pl.BlockSpec(memory_space=pl.ANY)
    f32 = jnp.float32
    dma = pltpu.SemaphoreType.DMA
    return pl.pallas_call(
        kernel,
        out_shape=(
            jax.ShapeDtypeStruct(layers_init.shape, f32),
            jax.ShapeDtypeStruct(residual_init.shape, f32),
        ),
        in_specs=[smem, smem, smem, hbm] + [vmem] * 7,
        out_specs=(hbm, vmem),
        scratch_shapes=[
            pltpu.VMEM((LAYERS, 8, 2048), f32),
            pltpu.VMEM((WIN, TILE), f32),
            pltpu.VMEM((LEAD + 7 * TD, TILE), f32),
            pltpu.VMEM((18, WIN - 8, TILE), f32),
            pltpu.VMEM((4 * WIN, TILE), f32),
            pltpu.VMEM((NS, PIECE, TILE), f32),
            pltpu.VMEM((NS, PIECE, TILE), f32),
            pltpu.VMEM((NS, PIECE, TILE), f32),
            pltpu.VMEM((4 * WIN + 8, TILE), f32),
            pltpu.VMEM((8, TILE), f32),
            pltpu.VMEM((NS, 8, TILE), f32),
            pltpu.VMEM((2, PIECE, TILE), f32),
            pltpu.VMEM((2, PIECE, TILE), f32),
            pltpu.VMEM((LAYERS, 2, 1, 2048), f32),
            pltpu.VMEM((2, LAYERS, 2, 1, 2048), f32),
            dma, dma((18,)), dma((18,)), dma((PARTS, NS)), dma((PARTS, NS)), dma((PARTS, NS)), dma((PARTS, NS)),
            dma((NS,)), dma((NS,)),
            dma((LAYERS, 2)), dma((2, LAYERS, 2)), dma((LAYERS, NS)), dma((LAYERS, NS)),
        ],
        compiler_params=pltpu.CompilerParams(
            collective_id=0, has_side_effects=True, vmem_limit_bytes=40 * 2**20
        ),
    )(foot_shift, omega, beta, layers_init, residual_init, wt_hi, wt_lo, w_hi, w_lo, m_hi, m_lo)


def solution(mesh):
    in_specs = (
        P(None, ("layer", "row"), None),
        P("sensor", ("layer", "row"), None),
        P("sensor", None),
        P("sensor", None, None, None, None),
        P(),
        P(),
        P(),
    )
    out_specs = (P(None, ("layer", "row"), None), P("sensor", ("layer", "row"), None))
    return jax.shard_map(
        per_device, mesh=mesh, in_specs=in_specs, out_specs=out_specs, check_vma=False
    )
```

```python
import functools

import jax
import jax.numpy as jnp
from jax import lax
from jax.experimental import pallas as pl
from jax.experimental.pallas import tpu as pltpu
from jax.sharding import PartitionSpec as P

MESH = pl.DeviceIdType.MESH
SWEEPS = 3
LAYERS = 4
NS = 8
NB = 32
ROWB = 4
TD = 128
TILE = 128
PIECE = 64
PARTS = 2
PART = PIECE // PARTS
SPAN = PART + 16
HALF = 72
WIN = 144
LEAD = 16
REACH = 3
ORDER = (4, 3, 5, 2, 6, 1, 7)
FROM = ((-3, -2, -1), (-3, -2, -1, 1, 2, 3), (-3, -2, -1, 1, 2, 3), (1, 2, 3))
SLOT0 = (0, 3, 9, 15)


def split(x):
    hi = x.astype(jnp.bfloat16)
    return hi, (x - hi.astype(jnp.float32)).astype(jnp.bfloat16)


def dot3(x, w_hi, w_lo):
    hi, lo = split(x)
    dot = functools.partial(jnp.dot, preferred_element_type=jnp.float32)
    return dot(hi, w_hi) + (dot(lo, w_hi) + dot(hi, w_lo))


def kernel(shift, omega, beta, layers_in, residual_in, wt_hi, wt_lo, w_hi, w_lo, m_hi, m_lo,
           layers_out, residual_out,
           field, win, frame, slots, flat, b_send, b_recv, c_send, halves_0, halves_1, out, par_send, par,
           lap, upd, halo_send, halo_recv,
           local_sem, slot_ssem, slot_rsem, b_ssem, b_rsem, c_ssem, c_rsem, p_ssem, p_rsem,
           h_ssem, h_rsem, f_ssem, f_rsem):
    lay, me, row = lax.axis_index("layer"), lax.axis_index("sensor"), lax.axis_index("row")
    block = lay * ROWB + row

    def at_block(dist):
        other = lax.rem(block + (dist + NB), NB)
        return (other // ROWB, me, lax.rem(other, ROWB))

    def at_sensor(dist):
        return (lay, lax.rem(me + dist, NS), row)

    first, last = me == 0, me == NS - 1
    up_block = lax.rem(block + NB - first.astype(jnp.int32), NB)
    down_block = lax.rem(block + last.astype(jnp.int32), NB)
    above = (up_block // ROWB, lax.rem(me + NS - 1, NS), lax.rem(up_block, ROWB))
    below = (down_block // ROWB, lax.rem(me + 1, NS), lax.rem(down_block, ROWB))

    barrier = pltpu.get_barrier_semaphore()
    partners = [at_sensor(d) for d in range(1, NS)]
    partners += [at_block(d) for d in (-3, -2, -1, 1, 2, 3)] + [above, below]
    load = pltpu.make_async_copy(layers_in.at[:, pl.ds(pl.multiple_of(me * 8, 8), 8), :], field, local_sem)
    load.start()
    frame[...] = jnp.zeros_like(frame)
    halves = (halves_0, halves_1)
    for buffer in halves:
        buffer[...] = jnp.zeros_like(buffer)
    win[pl.ds(0, LEAD), :] = jnp.zeros((LEAD, TILE), jnp.float32)
    win[pl.ds(LEAD, TD), :] = residual_in[0]
    odd = [lax.rem(shift[0, l], 2) for l in range(LAYERS)]
    half = [lax.rem(shift[0, l], 8) // 2 for l in range(LAYERS)]
    lag = [shift[0, l] // 8 for l in range(LAYERS)]
    for l in range(LAYERS):
        par_send[pl.ds(l, 1), :] = jnp.full((1, TILE), odd[l].astype(jnp.float32))
    par_send[pl.ds(LAYERS, 8 - LAYERS), :] = jnp.zeros((8 - LAYERS, TILE), jnp.float32)
    par[me] = par_send[...]
    load.wait()
    for other in partners:
        pl.semaphore_signal(barrier, inc=1, device_id=other, device_id_type=MESH)
    pl.semaphore_wait(barrier, len(partners))

    def par_copy(d):
        return pltpu.make_async_remote_copy(
            par_send, par.at[me], p_ssem.at[d], p_rsem.at[d], device_id=at_sensor(d), device_id_type=MESH)

    def halo_copies(l, slot):
        return [
            pltpu.make_async_remote_copy(
                halo_send.at[l, 0], halo_recv.at[slot, l, 1], h_ssem.at[l, 0], h_rsem.at[slot, l, 1],
                device_id=above, device_id_type=MESH),
            pltpu.make_async_remote_copy(
                halo_send.at[l, 1], halo_recv.at[slot, l, 0], h_ssem.at[l, 1], h_rsem.at[slot, l, 0],
                device_id=below, device_id_type=MESH),
        ]

    def halo_start(l, slot):
        halo_send[l, 0] = field[l, pl.ds(0, 1), :]
        halo_send[l, 1] = field[l, pl.ds(7, 1), :]
        for copy in halo_copies(l, slot):
            copy.start()

    for d in ORDER:
        par_copy(d).start()
    for l in range(LAYERS):
        halo_start(l, 0)

    def b_copy(d, q):
        part = pl.ds(PART * q, PART)
        return pltpu.make_async_remote_copy(
            b_send.at[d, part, :], b_recv.at[d, part, :], b_ssem.at[q, d], b_rsem.at[q, d], device_id=at_sensor(d), device_id_type=MESH)

    own_half = pl.ds(pl.multiple_of(SPAN * me + 8, 8), PART)

    def c_copy(d, q):
        return pltpu.make_async_remote_copy(
            c_send.at[d, pl.ds(PART * q, PART), :], halves[q].at[own_half, :], c_ssem.at[q, d], c_rsem.at[q, d],
            device_id=at_sensor(d), device_id_type=MESH)

    def f_copy(l, d):
        return pltpu.make_async_remote_copy(
            field.at[l], layers_out.at[l, pl.ds(pl.multiple_of(me * 8, 8), 8), :], f_ssem.at[l, d], f_rsem.at[l, d],
            device_id=at_sensor(d), device_id_type=MESH)

    def slot_copy(l, n, dist, q):
        n += SLOT0[l]
        return pltpu.make_async_remote_copy(
            out.at[q], slots.at[n, q], slot_ssem.at[q, n], slot_rsem.at[q, n],
            device_id=at_block(-dist), device_id_type=MESH)

    index = lax.broadcasted_iota(jnp.int32, (WIN, TILE), 0)
    line = lax.broadcasted_iota(jnp.int32, (HALF, TILE), 0)
    line = jnp.where(line < 64, 2 * line - (line & 7), 16 * line - 1025)
    cell_row = lax.broadcasted_iota(jnp.int32, (8, 2048), 0)
    cell_col = lax.broadcasted_iota(jnp.int32, (8, 2048), 1)
    at_top = jnp.logical_and(block == 0, first)
    at_bottom = jnp.logical_and(block == NB - 1, last)

    def step(sweep, l):
        start = LEAD + lag[l] - TD * block
        inside = index >= start
        products = dot3(jnp.where(inside, win[...], 0.0), wt_hi[l], wt_lo[l])
        for k in range(4):
            flat[pl.ds(k, WIN, stride=4), :] = products[:, k * TILE:(k + 1) * TILE]
        for q in range(PARTS):
            for d in ORDER:
                to = lax.rem(me + d, NS)
                b_send[d, pl.ds(PART * q, PART), :] = flat[pl.ds(64 + PIECE * to + PART * q - half[l], PART), :]
                b_copy(d, q).start()
        own = flat[pl.ds(64 + PIECE * me - half[l], PIECE), :]
        slot = lax.rem(sweep, 2)
        for copy in halo_copies(l, slot):
            copy.wait_recv()
        f = field[l]
        top = jnp.where(at_top, 0.0, halo_recv[slot, l, 0])
        bottom = jnp.where(at_bottom, 0.0, halo_recv[slot, l, 1])
        north = jnp.where(cell_row == 0, top, pltpu.roll(f, 1, 0))
        south = jnp.where(cell_row == 7, bottom, pltpu.roll(f, 7, 0))
        west = jnp.where(cell_col == 0, 0.0, pltpu.roll(f, 1, 1))
        east = jnp.where(cell_col == 2047, 0.0, pltpu.roll(f, 2047, 1))
        laplace = 4.0 * f - north - south - west - east

        if l == 0:
            @pl.when(sweep == 0)
            def _():
                for d in ORDER:
                    par_copy(d).wait_recv()

        weight = -beta[l]
        for c in range(16):
            lap[c % 2, pl.ds(c // 2, 8, stride=8), :] = weight * laplace[:, c * TILE:(c + 1) * TILE]
        is_odd = par[me, pl.ds(l, 1), :] > 0.5
        is_odd_from = {d: par[lax.rem(me + (NS - d), NS), pl.ds(l, 1), :] > 0.5 for d in ORDER}
        is_odd_to = {d: is_odd_from[NS - d] for d in ORDER}
        for q in range(PARTS):
            part = pl.ds(PART * q, PART)
            mine = own[PART * q:PART * (q + 1)]
            even_sum = lap[0, part, :] + jnp.where(is_odd, 0.0, mine)
            odd_sum = lap[1, part, :] + jnp.where(is_odd, mine, 0.0)
            for d in reversed(ORDER):
                b_copy(d, q).wait_recv()
                piece = b_recv[d, part, :]
                even_sum = even_sum + jnp.where(is_odd_from[d], 0.0, piece)
                odd_sum = odd_sum + jnp.where(is_odd_from[d], piece, 0.0)
            update = omega[l] * dot3(jnp.concatenate([even_sum, odd_sum], axis=0), m_hi[l], m_lo[l])
            even, odd_ = update[:PART], update[PART:]
            for d in ORDER:
                c_send[d, part, :] = jnp.where(is_odd_to[d], odd_, even)
                c_copy(d, q).start()
            upd[0, part, :] = even
            upd[1, part, :] = odd_
            halves[q][own_half, :] = jnp.where(is_odd, odd_, even)
        for c in range(16):
            field[l, :, c * TILE:(c + 1) * TILE] = (
                f[:, c * TILE:(c + 1) * TILE] + upd[c % 2, pl.ds(c // 2, 8, stride=8), :])
        for copy in halo_copies(l, slot):
            copy.wait_send()

        @pl.when(sweep < SWEEPS - 1)
        def _():
            halo_start(l, 1 - slot)

        @pl.when(sweep == SWEEPS - 1)
        def _():
            for d in ORDER:
                f_copy(l, d).start()

        for q in range(PARTS):
            for d in ORDER:
                b_copy(d, q).wait_send()
        none = jnp.zeros((8, TILE), jnp.float32)
        for q in range(PARTS):
            for d in ORDER:
                c_copy(d, q).wait_recv()
            columns = []
            for k in range(4):
                at = half[l] + k
                groups = [halves[q][pl.ds(SPAN * p + 8 + at, 8, stride=4), :] for p in range(8)]
                groups += [halves[q][pl.ds(4 + at, 8, stride=SPAN), :], none]
                columns.append(jnp.concatenate(groups, axis=0))
            change = dot3(jnp.concatenate(columns, axis=1), w_hi[l], w_lo[l])[:HALF]
            old = jnp.concatenate([win[pl.ds(LEAD + 16 * p + 8 * q, 8), :] for p in range(8)] + [none], axis=0)
            out[q] = old - jnp.where(line + (LEAD + 8 * q) >= start, change, 0.0)
            for n, dist in enumerate(FROM[l]):
                slot_copy(l, n, dist, q).start()
        for q in range(PARTS):
            for d in ORDER:
                c_copy(d, q).wait_send()

    def reframe(l):
        sources = FROM[l]
        least = min(sources[0], 0)
        base = -least * TD
        views = [(base, out)] + [(base + dist * TD, slots.at[SLOT0[l] + n]) for n, dist in enumerate(sources)]

        def place(at, view, q):
            for p in range(8):
                frame[pl.ds(LEAD + at + 16 * p + 8 * q, 8), :] = view[q, pl.ds(8 * p, 8), :]

        frame[pl.ds(0, LEAD), :] = jnp.zeros((LEAD, TILE), jnp.float32)
        for q in range(PARTS):
            place(*views[0], q)
        for q in range(PARTS):
            for n, dist in enumerate(sources):
                slot_copy(l, n, dist, q).wait_recv()
                place(*views[1 + n], q)
        for at, view in views:
            for q in range(PARTS):
                rows = pl.ds(LEAD - 1 + at + 8 * q, 8, stride=16)
                frame[rows, :] = frame[rows, :] + view[q, pl.ds(64, 8), :]
        moved = frame[pl.ds(base + lag[l] - lag[(l + 1) % LAYERS], WIN), :]
        for q in range(PARTS):
            for n, dist in enumerate(sources):
                slot_copy(l, n, dist, q).wait_send()
        win[...] = moved

    def turn(sweep, carry):
        for l in range(LAYERS):
            step(sweep, l)
            reframe(l)
        return carry

    lax.fori_loop(0, SWEEPS, turn, 0)
    residual_out[0] = win[pl.ds(LEAD, TD), :]
    store = pltpu.make_async_copy(field, layers_out.at[:, pl.ds(pl.multiple_of(me * 8, 8), 8), :], local_sem)
    store.start()
    for d in ORDER:
        par_copy(d).wait_send()
    for l in range(LAYERS):
        for d in ORDER:
            f_copy(l, d).wait()
    store.wait()


def halves_of(x):
    hi = lax.reduce_precision(x, exponent_bits=8, mantissa_bits=7)
    return hi.astype(jnp.bfloat16), (x - hi).astype(jnp.bfloat16)


def per_device(layers_init, residual_init, foot_shift, blocks, precond, omega, beta):
    w = blocks[0]
    w_hi, w_lo = halves_of(w.reshape(LAYERS, 4 * TILE, TILE))
    wt_hi, wt_lo = halves_of(jnp.transpose(w, (0, 3, 1, 2)).reshape(LAYERS, TILE, 4 * TILE))
    m_hi, m_lo = halves_of(precond)
    smem = pl.BlockSpec(memory_space=pltpu.SMEM)
    vmem = pl.BlockSpec(memory_space=pltpu.VMEM)
    hbm = pl.BlockSpec(memory_space=pl.ANY)
    f32 = jnp.float32
    dma = pltpu.SemaphoreType.DMA
    return pl.pallas_call(
        kernel,
        out_shape=(
            jax.ShapeDtypeStruct(layers_init.shape, f32),
            jax.ShapeDtypeStruct(residual_init.shape, f32),
        ),
        in_specs=[smem, smem, smem, hbm] + [vmem] * 7,
        out_specs=(hbm, vmem),
        scratch_shapes=[
            pltpu.VMEM((LAYERS, 8, 2048), f32),
            pltpu.VMEM((WIN, TILE), f32),
            pltpu.VMEM((LEAD + 7 * TD, TILE), f32),
            pltpu.VMEM((18, PARTS, HALF, TILE), f32),
            pltpu.VMEM((4 * WIN, TILE), f32),
            pltpu.VMEM((NS, PIECE, TILE), f32),
            pltpu.VMEM((NS, PIECE, TILE), f32),
            pltpu.VMEM((NS, PIECE, TILE), f32),
            pltpu.VMEM((8 * SPAN, TILE), f32),
            pltpu.VMEM((8 * SPAN, TILE), f32),
            pltpu.VMEM((PARTS, HALF, TILE), f32),
            pltpu.VMEM((8, TILE), f32),
            pltpu.VMEM((NS, 8, TILE), f32),
            pltpu.VMEM((2, PIECE, TILE), f32),
            pltpu.VMEM((2, PIECE, TILE), f32),
            pltpu.VMEM((LAYERS, 2, 1, 2048), f32),
            pltpu.VMEM((2, LAYERS, 2, 1, 2048), f32),
            dma, dma((PARTS, 18)), dma((PARTS, 18)), dma((PARTS, NS)), dma((PARTS, NS)), dma((PARTS, NS)), dma((PARTS, NS)),
            dma((NS,)), dma((NS,)),
            dma((LAYERS, 2)), dma((2, LAYERS, 2)), dma((LAYERS, NS)), dma((LAYERS, NS)),
        ],
        compiler_params=pltpu.CompilerParams(
            collective_id=0, has_side_effects=True, vmem_limit_bytes=40 * 2**20
        ),
    )(foot_shift, omega, beta, layers_init, residual_init, wt_hi, wt_lo, w_hi, w_lo, m_hi, m_lo)


def solution(mesh):
    in_specs = (
        P(None, ("layer", "row"), None),
        P("sensor", ("layer", "row"), None),
        P("sensor", None),
        P("sensor", None, None, None, None),
        P(),
        P(),
        P(),
    )
    out_specs = (P(None, ("layer", "row"), None), P("sensor", ("layer", "row"), None))
    return jax.shard_map(
        per_device, mesh=mesh, in_specs=in_specs, out_specs=out_specs, check_vma=False
    )
```

```python
import functools

import jax
import jax.numpy as jnp
from jax import lax
from jax.experimental import pallas as pl
from jax.experimental.pallas import tpu as pltpu
from jax.sharding import PartitionSpec as P

MESH = pl.DeviceIdType.MESH
SWEEPS = 3
LAYERS = 4
NS = 8
NB = 32
ROWB = 4
TD = 128
TILE = 128
PIECE = 64
PARTS = 2
PART = PIECE // PARTS
SPAN = PART + 16
HALF = 72
WIN = 144
LEAD = 16
REACH = 3
ORDER = (4, 3, 5, 2, 6, 1, 7)
FROM = ((-3, -2, -1), (-3, -2, -1, 1, 2, 3), (-3, -2, -1, 1, 2, 3), (1, 2, 3))
SLOT0 = (0, 3, 9, 15)


def split(x):
    hi = x.astype(jnp.bfloat16)
    return hi, (x - hi.astype(jnp.float32)).astype(jnp.bfloat16)


def dot3(x, w_hi, w_lo):
    hi, lo = split(x)
    dot = functools.partial(jnp.dot, preferred_element_type=jnp.float32)
    return dot(hi, w_hi) + (dot(lo, w_hi) + dot(hi, w_lo))


def kernel(shift, omega, beta, layers_in, residual_in, blocks_in, precond_in,
           layers_out, residual_out,
           raw, raw_m, wt_hi, wt_lo, w_hi, w_lo, m_hi, m_lo,
           field, win, frame, slots, flat, b_send, b_recv, c_send, halves_0, halves_1, out, par_send, par,
           lap, upd, halo_send, halo_recv,
           local_sem, slot_ssem, slot_rsem, b_ssem, b_rsem, c_ssem, c_rsem, p_ssem, p_rsem,
           h_ssem, h_rsem, f_ssem, f_rsem):
    lay, me, row = lax.axis_index("layer"), lax.axis_index("sensor"), lax.axis_index("row")
    block = lay * ROWB + row

    def at_block(dist):
        other = lax.rem(block + (dist + NB), NB)
        return (other // ROWB, me, lax.rem(other, ROWB))

    def at_sensor(dist):
        return (lay, lax.rem(me + dist, NS), row)

    first, last = me == 0, me == NS - 1
    up_block = lax.rem(block + NB - first.astype(jnp.int32), NB)
    down_block = lax.rem(block + last.astype(jnp.int32), NB)
    above = (up_block // ROWB, lax.rem(me + NS - 1, NS), lax.rem(up_block, ROWB))
    below = (down_block // ROWB, lax.rem(me + 1, NS), lax.rem(down_block, ROWB))

    barrier = pltpu.get_barrier_semaphore()
    partners = [at_sensor(d) for d in range(1, NS)]
    partners += [at_block(d) for d in (-3, -2, -1, 1, 2, 3)] + [above, below]
    for other in partners:
        pl.semaphore_signal(barrier, inc=1, device_id=other, device_id_type=MESH)

    own_rows = pl.ds(pl.multiple_of(me * 8, 8), 8)
    loads = [
        pltpu.make_async_copy(blocks_in.at[0, 0], raw.at[0], local_sem.at[0]),
        pltpu.make_async_copy(precond_in, raw_m, local_sem.at[1]),
        pltpu.make_async_copy(residual_in.at[0], win.at[pl.ds(LEAD, TD), :], local_sem.at[2]),
        pltpu.make_async_copy(layers_in.at[:, own_rows, :], field, local_sem.at[3]),
    ] + [pltpu.make_async_copy(blocks_in.at[0, l], raw.at[l], local_sem.at[3 + l]) for l in range(1, LAYERS)]
    for load in loads:
        load.start()
    frame[...] = jnp.zeros_like(frame)
    halves = (halves_0, halves_1)
    for buffer in halves:
        buffer[...] = jnp.zeros_like(buffer)
    win[pl.ds(0, LEAD), :] = jnp.zeros((LEAD, TILE), jnp.float32)
    odd = [lax.rem(shift[0, l], 2) for l in range(LAYERS)]
    half = [lax.rem(shift[0, l], 8) // 2 for l in range(LAYERS)]
    lag = [shift[0, l] // 8 for l in range(LAYERS)]
    for l in range(LAYERS):
        par_send[pl.ds(l, 1), :] = jnp.full((1, TILE), odd[l].astype(jnp.float32))
    par_send[pl.ds(LAYERS, 8 - LAYERS), :] = jnp.zeros((8 - LAYERS, TILE), jnp.float32)

    def prepare(l):
        m_hi[l], m_lo[l] = split(raw_m[l])
        for k in range(4):
            rows = pl.ds(k * TILE, TILE)
            block_k = raw[l, k]
            w_hi[l, rows, :], w_lo[l, rows, :] = split(block_k)
            wt_hi[l, :, k * TILE:(k + 1) * TILE], wt_lo[l, :, k * TILE:(k + 1) * TILE] = split(block_k.T)

    for load in loads[:2]:
        load.wait()
    prepare(0)
    for load in loads[2:4]:
        load.wait()
    for l in range(LAYERS):
        halo_send[l, 0] = field[l, pl.ds(0, 1), :]
        halo_send[l, 1] = field[l, pl.ds(7, 1), :]
    pl.semaphore_wait(barrier, len(partners))

    def par_copy(d):
        return pltpu.make_async_remote_copy(
            par_send, par.at[me], p_ssem.at[d], p_rsem.at[d], device_id=at_sensor(d), device_id_type=MESH)

    def halo_copies(l, slot):
        return [
            pltpu.make_async_remote_copy(
                halo_send.at[l, 0], halo_recv.at[slot, l, 1], h_ssem.at[l, 0], h_rsem.at[slot, l, 1],
                device_id=above, device_id_type=MESH),
            pltpu.make_async_remote_copy(
                halo_send.at[l, 1], halo_recv.at[slot, l, 0], h_ssem.at[l, 1], h_rsem.at[slot, l, 0],
                device_id=below, device_id_type=MESH),
        ]

    def halo_start(l, slot):
        halo_send[l, 0] = field[l, pl.ds(0, 1), :]
        halo_send[l, 1] = field[l, pl.ds(7, 1), :]
        for copy in halo_copies(l, slot):
            copy.start()

    for d in ORDER:
        par_copy(d).start()
    for l in range(LAYERS):
        for copy in halo_copies(l, 0):
            copy.start()

    def b_copy(d, q):
        part = pl.ds(PART * q, PART)
        return pltpu.make_async_remote_copy(
            b_send.at[d, part, :], b_recv.at[d, part, :], b_ssem.at[q, d], b_rsem.at[q, d], device_id=at_sensor(d), device_id_type=MESH)

    own_half = pl.ds(pl.multiple_of(SPAN * me + 8, 8), PART)

    def c_copy(d, q):
        return pltpu.make_async_remote_copy(
            c_send.at[d, pl.ds(PART * q, PART), :], halves[q].at[own_half, :], c_ssem.at[q, d], c_rsem.at[q, d],
            device_id=at_sensor(d), device_id_type=MESH)

    def f_copy(l, d):
        return pltpu.make_async_remote_copy(
            field.at[l], layers_out.at[l, pl.ds(pl.multiple_of(me * 8, 8), 8), :], f_ssem.at[l, d], f_rsem.at[l, d],
            device_id=at_sensor(d), device_id_type=MESH)

    def slot_copy(l, n, dist, q):
        n += SLOT0[l]
        return pltpu.make_async_remote_copy(
            out.at[q], slots.at[n, q], slot_ssem.at[q, n], slot_rsem.at[q, n],
            device_id=at_block(-dist), device_id_type=MESH)

    index = lax.broadcasted_iota(jnp.int32, (WIN, TILE), 0)
    line = lax.broadcasted_iota(jnp.int32, (HALF, TILE), 0)
    line = jnp.where(line < 64, 2 * line - (line & 7), 16 * line - 1025)
    cell_row = lax.broadcasted_iota(jnp.int32, (8, 2048), 0)
    cell_col = lax.broadcasted_iota(jnp.int32, (8, 2048), 1)
    at_top = jnp.logical_and(block == 0, first)
    at_bottom = jnp.logical_and(block == NB - 1, last)

    def step(sweep, l):
        start = LEAD + lag[l] - TD * block
        inside = index >= start
        products = dot3(jnp.where(inside, win[...], 0.0), wt_hi[l], wt_lo[l])
        for k in range(4):
            flat[pl.ds(k, WIN, stride=4), :] = products[:, k * TILE:(k + 1) * TILE]
        for q in range(PARTS):
            for d in ORDER:
                to = lax.rem(me + d, NS)
                b_send[d, pl.ds(PART * q, PART), :] = flat[pl.ds(64 + PIECE * to + PART * q - half[l], PART), :]
                b_copy(d, q).start()
        own = flat[pl.ds(64 + PIECE * me - half[l], PIECE), :]
        if l == 0:
            @pl.when(sweep == 0)
            def _():
                for other in range(1, LAYERS):
                    loads[3 + other].wait()
                    prepare(other)
        slot = lax.rem(sweep, 2)
        for copy in halo_copies(l, slot):
            copy.wait_recv()
        f = field[l]
        top = jnp.where(at_top, 0.0, halo_recv[slot, l, 0])
        bottom = jnp.where(at_bottom, 0.0, halo_recv[slot, l, 1])
        north = jnp.where(cell_row == 0, top, pltpu.roll(f, 1, 0))
        south = jnp.where(cell_row == 7, bottom, pltpu.roll(f, 7, 0))
        west = jnp.where(cell_col == 0, 0.0, pltpu.roll(f, 1, 1))
        east = jnp.where(cell_col == 2047, 0.0, pltpu.roll(f, 2047, 1))
        laplace = 4.0 * f - north - south - west - east

        if l == 0:
            @pl.when(sweep == 0)
            def _():
                for d in ORDER:
                    par_copy(d).wait_recv()

        weight = -beta[l]
        for c in range(16):
            lap[c % 2, pl.ds(c // 2, 8, stride=8), :] = weight * laplace[:, c * TILE:(c + 1) * TILE]
        is_odd = par_send[pl.ds(l, 1), :] > 0.5
        is_odd_from = {d: par[lax.rem(me + (NS - d), NS), pl.ds(l, 1), :] > 0.5 for d in ORDER}
        is_odd_to = {d: is_odd_from[NS - d] for d in ORDER}
        for q in range(PARTS):
            part = pl.ds(PART * q, PART)
            mine = own[PART * q:PART * (q + 1)]
            even_sum = lap[0, part, :] + jnp.where(is_odd, 0.0, mine)
            odd_sum = lap[1, part, :] + jnp.where(is_odd, mine, 0.0)
            for d in reversed(ORDER):
                b_copy(d, q).wait_recv()
                piece = b_recv[d, part, :]
                even_sum = even_sum + jnp.where(is_odd_from[d], 0.0, piece)
                odd_sum = odd_sum + jnp.where(is_odd_from[d], piece, 0.0)
            update = omega[l] * dot3(jnp.concatenate([even_sum, odd_sum], axis=0), m_hi[l], m_lo[l])
            even, odd_ = update[:PART], update[PART:]
            for d in ORDER:
                c_send[d, part, :] = jnp.where(is_odd_to[d], odd_, even)
                c_copy(d, q).start()
            upd[0, part, :] = even
            upd[1, part, :] = odd_
            halves[q][own_half, :] = jnp.where(is_odd, odd_, even)
        for c in range(16):
            field[l, :, c * TILE:(c + 1) * TILE] = (
                f[:, c * TILE:(c + 1) * TILE] + upd[c % 2, pl.ds(c // 2, 8, stride=8), :])
        for copy in halo_copies(l, slot):
            copy.wait_send()

        @pl.when(sweep < SWEEPS - 1)
        def _():
            halo_start(l, 1 - slot)

        @pl.when(sweep == SWEEPS - 1)
        def _():
            for d in ORDER:
                f_copy(l, d).start()

        for q in range(PARTS):
            for d in ORDER:
                b_copy(d, q).wait_send()
        none = jnp.zeros((8, TILE), jnp.float32)
        for q in range(PARTS):
            for d in ORDER:
                c_copy(d, q).wait_recv()
            columns = []
            for k in range(4):
                at = half[l] + k
                groups = [halves[q][pl.ds(SPAN * p + 8 + at, 8, stride=4), :] for p in range(8)]
                groups += [halves[q][pl.ds(4 + at, 8, stride=SPAN), :], none]
                columns.append(jnp.concatenate(groups, axis=0))
            change = dot3(jnp.concatenate(columns, axis=1), w_hi[l], w_lo[l])[:HALF]
            old = jnp.concatenate([win[pl.ds(LEAD + 16 * p + 8 * q, 8), :] for p in range(8)] + [none], axis=0)
            out[q] = old - jnp.where(line + (LEAD + 8 * q) >= start, change, 0.0)
            for n, dist in enumerate(FROM[l]):
                slot_copy(l, n, dist, q).start()
        for q in range(PARTS):
            for d in ORDER:
                c_copy(d, q).wait_send()

    def reframe(l):
        sources = FROM[l]
        least = min(sources[0], 0)
        base = -least * TD
        views = [(base, out)] + [(base + dist * TD, slots.at[SLOT0[l] + n]) for n, dist in enumerate(sources)]

        def place(at, view, q):
            for p in range(8):
                frame[pl.ds(LEAD + at + 16 * p + 8 * q, 8), :] = view[q, pl.ds(8 * p, 8), :]

        frame[pl.ds(0, LEAD), :] = jnp.zeros((LEAD, TILE), jnp.float32)
        for q in range(PARTS):
            place(*views[0], q)
        for q in range(PARTS):
            for n, dist in enumerate(sources):
                slot_copy(l, n, dist, q).wait_recv()
                place(*views[1 + n], q)
        for at, view in views:
            for q in range(PARTS):
                rows = pl.ds(LEAD - 1 + at + 8 * q, 8, stride=16)
                frame[rows, :] = frame[rows, :] + view[q, pl.ds(64, 8), :]
        moved = frame[pl.ds(base + lag[l] - lag[(l + 1) % LAYERS], WIN), :]
        for q in range(PARTS):
            for n, dist in enumerate(sources):
                slot_copy(l, n, dist, q).wait_send()
        win[...] = moved

    def turn(sweep, carry):
        for l in range(LAYERS):
            step(sweep, l)
            reframe(l)
        return carry

    lax.fori_loop(0, SWEEPS, turn, 0)
    residual_out[0] = win[pl.ds(LEAD, TD), :]
    store = pltpu.make_async_copy(field, layers_out.at[:, own_rows, :], local_sem.at[0])
    store.start()
    for d in ORDER:
        par_copy(d).wait_send()
    for l in range(LAYERS):
        for d in ORDER:
            f_copy(l, d).wait()
    store.wait()


def per_device(layers_init, residual_init, foot_shift, blocks, precond, omega, beta):
    smem = pl.BlockSpec(memory_space=pltpu.SMEM)
    vmem = pl.BlockSpec(memory_space=pltpu.VMEM)
    hbm = pl.BlockSpec(memory_space=pl.ANY)
    f32, bf16 = jnp.float32, jnp.bfloat16
    dma = pltpu.SemaphoreType.DMA
    return pl.pallas_call(
        kernel,
        out_shape=(
            jax.ShapeDtypeStruct(layers_init.shape, f32),
            jax.ShapeDtypeStruct(residual_init.shape, f32),
        ),
        in_specs=[smem] * 3 + [hbm] * 4,
        out_specs=(hbm, vmem),
        scratch_shapes=[
            pltpu.VMEM((LAYERS, 4, TILE, TILE), f32),
            pltpu.VMEM((LAYERS, TILE, TILE), f32),
            pltpu.VMEM((LAYERS, TILE, 4 * TILE), bf16),
            pltpu.VMEM((LAYERS, TILE, 4 * TILE), bf16),
            pltpu.VMEM((LAYERS, 4 * TILE, TILE), bf16),
            pltpu.VMEM((LAYERS, 4 * TILE, TILE), bf16),
            pltpu.VMEM((LAYERS, TILE, TILE), bf16),
            pltpu.VMEM((LAYERS, TILE, TILE), bf16),
            pltpu.VMEM((LAYERS, 8, 2048), f32),
            pltpu.VMEM((WIN, TILE), f32),
            pltpu.VMEM((LEAD + 7 * TD, TILE), f32),
            pltpu.VMEM((18, PARTS, HALF, TILE), f32),
            pltpu.VMEM((4 * WIN, TILE), f32),
            pltpu.VMEM((NS, PIECE, TILE), f32),
            pltpu.VMEM((NS, PIECE, TILE), f32),
            pltpu.VMEM((NS, PIECE, TILE), f32),
            pltpu.VMEM((8 * SPAN, TILE), f32),
            pltpu.VMEM((8 * SPAN, TILE), f32),
            pltpu.VMEM((PARTS, HALF, TILE), f32),
            pltpu.VMEM((8, TILE), f32),
            pltpu.VMEM((NS, 8, TILE), f32),
            pltpu.VMEM((2, PIECE, TILE), f32),
            pltpu.VMEM((2, PIECE, TILE), f32),
            pltpu.VMEM((LAYERS, 2, 1, 2048), f32),
            pltpu.VMEM((2, LAYERS, 2, 1, 2048), f32),
            dma((7,)), dma((PARTS, 18)), dma((PARTS, 18)), dma((PARTS, NS)), dma((PARTS, NS)), dma((PARTS, NS)), dma((PARTS, NS)),
            dma((NS,)), dma((NS,)),
            dma((LAYERS, 2)), dma((2, LAYERS, 2)), dma((LAYERS, NS)), dma((LAYERS, NS)),
        ],
        compiler_params=pltpu.CompilerParams(
            collective_id=0, has_side_effects=True, vmem_limit_bytes=40 * 2**20
        ),
    )(foot_shift, omega, beta, layers_init, residual_init, blocks, precond)


def solution(mesh):
    in_specs = (
        P(None, ("layer", "row"), None),
        P("sensor", ("layer", "row"), None),
        P("sensor", None),
        P("sensor", None, None, None, None),
        P(),
        P(),
        P(),
    )
    out_specs = (P(None, ("layer", "row"), None), P("sensor", ("layer", "row"), None))
    return jax.shard_map(
        per_device, mesh=mesh, in_specs=in_specs, out_specs=out_specs, check_vma=False
    )
```

```python
import functools

import jax
import jax.numpy as jnp
from jax import lax
from jax.experimental import pallas as pl
from jax.experimental.pallas import tpu as pltpu
from jax.sharding import PartitionSpec as P

MESH = pl.DeviceIdType.MESH
SWEEPS = 3
LAYERS = 4
NS = 8
NB = 32
ROWB = 4
TD = 128
TILE = 128
PIECE = 64
PARTS = 2
PART = PIECE // PARTS
SPAN = PART + 16
HALF = 72
WIN = 144
LEAD = 16
REACH = 3
ORDER = (4, 3, 5, 2, 6, 1, 7)
FROM = ((-3, -2, -1), (-3, -2, -1, 1, 2, 3), (-3, -2, -1, 1, 2, 3), (1, 2, 3))
SLOT0 = (0, 3, 9, 15)


def split(x):
    hi = x.astype(jnp.bfloat16)
    return hi, (x - hi.astype(jnp.float32)).astype(jnp.bfloat16)


def dot3(x, w_hi, w_lo):
    hi, lo = split(x)
    dot = functools.partial(jnp.dot, preferred_element_type=jnp.float32)
    return dot(hi, w_hi) + (dot(lo, w_hi) + dot(hi, w_lo))


def kernel(shift_in, omega_in, beta_in, layers_in, residual_in, blocks_in, precond_in,
           layers_out, residual_out,
           shift, omega, beta, raw, raw_m, wt_hi, wt_lo, w_hi, w_lo, m_hi, m_lo,
           field, win, frame, slots, flat, b_send, b_recv, c_send, halves_0, halves_1, out, par_send, par,
           lap, upd, halo_send, halo_recv,
           local_sem, slot_ssem, slot_rsem, b_ssem, b_rsem, c_ssem, c_rsem, p_ssem, p_rsem,
           h_ssem, h_rsem, f_ssem, f_rsem):
    lay, me, row = lax.axis_index("layer"), lax.axis_index("sensor"), lax.axis_index("row")
    block = lay * ROWB + row

    def at_block(dist):
        other = lax.rem(block + (dist + NB), NB)
        return (other // ROWB, me, lax.rem(other, ROWB))

    def at_sensor(dist):
        return (lay, lax.rem(me + dist, NS), row)

    first, last = me == 0, me == NS - 1
    up_block = lax.rem(block + NB - first.astype(jnp.int32), NB)
    down_block = lax.rem(block + last.astype(jnp.int32), NB)
    above = (up_block // ROWB, lax.rem(me + NS - 1, NS), lax.rem(up_block, ROWB))
    below = (down_block // ROWB, lax.rem(me + 1, NS), lax.rem(down_block, ROWB))

    barrier = pltpu.get_barrier_semaphore()
    partners = [at_sensor(d) for d in range(1, NS)]
    partners += [at_block(d) for d in (-3, -2, -1, 1, 2, 3)] + [above, below]
    for other in partners:
        pl.semaphore_signal(barrier, inc=1, device_id=other, device_id_type=MESH)

    own_rows = pl.ds(pl.multiple_of(me * 8, 8), 8)
    scalars = [
        pltpu.make_async_copy(shift_in, shift, local_sem.at[7]),
        pltpu.make_async_copy(omega_in, omega, local_sem.at[8]),
        pltpu.make_async_copy(beta_in, beta, local_sem.at[9]),
    ]
    for load in scalars:
        load.start()
    loads = [
        pltpu.make_async_copy(blocks_in.at[0, 0], raw.at[0], local_sem.at[0]),
        pltpu.make_async_copy(precond_in, raw_m, local_sem.at[1]),
        pltpu.make_async_copy(residual_in.at[0], win.at[pl.ds(LEAD, TD), :], local_sem.at[2]),
        pltpu.make_async_copy(layers_in.at[:, own_rows, :], field, local_sem.at[3]),
    ] + [pltpu.make_async_copy(blocks_in.at[0, l], raw.at[l], local_sem.at[3 + l]) for l in range(1, LAYERS)]
    for load in loads:
        load.start()
    frame[...] = jnp.zeros_like(frame)
    halves = (halves_0, halves_1)
    for buffer in halves:
        buffer[...] = jnp.zeros_like(buffer)
    win[pl.ds(0, LEAD), :] = jnp.zeros((LEAD, TILE), jnp.float32)
    for load in scalars:
        load.wait()
    odd = [lax.rem(shift[0, l], 2) for l in range(LAYERS)]
    half = [lax.rem(shift[0, l], 8) // 2 for l in range(LAYERS)]
    lag = [shift[0, l] // 8 for l in range(LAYERS)]
    for l in range(LAYERS):
        par_send[pl.ds(l, 1), :] = jnp.full((1, TILE), odd[l].astype(jnp.float32))
    par_send[pl.ds(LAYERS, 8 - LAYERS), :] = jnp.zeros((8 - LAYERS, TILE), jnp.float32)

    def prepare(l):
        m_hi[l], m_lo[l] = split(raw_m[l])
        for k in range(4):
            rows = pl.ds(k * TILE, TILE)
            block_k = raw[l, k]
            w_hi[l, rows, :], w_lo[l, rows, :] = split(block_k)
            wt_hi[l, :, k * TILE:(k + 1) * TILE], wt_lo[l, :, k * TILE:(k + 1) * TILE] = split(block_k.T)

    for load in loads[:2]:
        load.wait()
    prepare(0)
    for load in loads[2:4]:
        load.wait()
    for l in range(LAYERS):
        halo_send[l, 0] = field[l, pl.ds(0, 1), :]
        halo_send[l, 1] = field[l, pl.ds(7, 1), :]
    pl.semaphore_wait(barrier, len(partners))

    def par_copy(d):
        return pltpu.make_async_remote_copy(
            par_send, par.at[me], p_ssem.at[d], p_rsem.at[d], device_id=at_sensor(d), device_id_type=MESH)

    def halo_copies(l, slot):
        return [
            pltpu.make_async_remote_copy(
                halo_send.at[l, 0], halo_recv.at[slot, l, 1], h_ssem.at[l, 0], h_rsem.at[slot, l, 1],
                device_id=above, device_id_type=MESH),
            pltpu.make_async_remote_copy(
                halo_send.at[l, 1], halo_recv.at[slot, l, 0], h_ssem.at[l, 1], h_rsem.at[slot, l, 0],
                device_id=below, device_id_type=MESH),
        ]

    def halo_start(l, slot):
        halo_send[l, 0] = field[l, pl.ds(0, 1), :]
        halo_send[l, 1] = field[l, pl.ds(7, 1), :]
        for copy in halo_copies(l, slot):
            copy.start()

    for d in ORDER:
        par_copy(d).start()
    for l in range(LAYERS):
        for copy in halo_copies(l, 0):
            copy.start()

    def b_copy(d, q):
        part = pl.ds(PART * q, PART)
        return pltpu.make_async_remote_copy(
            b_send.at[d, part, :], b_recv.at[d, part, :], b_ssem.at[q, d], b_rsem.at[q, d], device_id=at_sensor(d), device_id_type=MESH)

    own_half = pl.ds(pl.multiple_of(SPAN * me + 8, 8), PART)

    def c_copy(d, q):
        return pltpu.make_async_remote_copy(
            c_send.at[d, pl.ds(PART * q, PART), :], halves[q].at[own_half, :], c_ssem.at[q, d], c_rsem.at[q, d],
            device_id=at_sensor(d), device_id_type=MESH)

    def f_copy(l, d):
        return pltpu.make_async_remote_copy(
            field.at[l], layers_out.at[l, pl.ds(pl.multiple_of(me * 8, 8), 8), :], f_ssem.at[l, d], f_rsem.at[l, d],
            device_id=at_sensor(d), device_id_type=MESH)

    def slot_copy(l, n, dist, q):
        n += SLOT0[l]
        return pltpu.make_async_remote_copy(
            out.at[q], slots.at[n, q], slot_ssem.at[q, n], slot_rsem.at[q, n],
            device_id=at_block(-dist), device_id_type=MESH)

    index = lax.broadcasted_iota(jnp.int32, (WIN, TILE), 0)
    line = lax.broadcasted_iota(jnp.int32, (HALF, TILE), 0)
    line = jnp.where(line < 64, 2 * line - (line & 7), 16 * line - 1025)
    cell_row = lax.broadcasted_iota(jnp.int32, (8, 2048), 0)
    cell_col = lax.broadcasted_iota(jnp.int32, (8, 2048), 1)
    at_top = jnp.logical_and(block == 0, first)
    at_bottom = jnp.logical_and(block == NB - 1, last)

    def step(sweep, l):
        start = LEAD + lag[l] - TD * block
        inside = index >= start
        products = dot3(jnp.where(inside, win[...], 0.0), wt_hi[l], wt_lo[l])
        for k in range(4):
            flat[pl.ds(k, WIN, stride=4), :] = products[:, k * TILE:(k + 1) * TILE]
        for q in range(PARTS):
            for d in ORDER:
                to = lax.rem(me + d, NS)
                b_send[d, pl.ds(PART * q, PART), :] = flat[pl.ds(64 + PIECE * to + PART * q - half[l], PART), :]
                b_copy(d, q).start()
        own = flat[pl.ds(64 + PIECE * me - half[l], PIECE), :]
        if l == 0:
            @pl.when(sweep == 0)
            def _():
                for other in range(1, LAYERS):
                    loads[3 + other].wait()
                    prepare(other)
        slot = lax.rem(sweep, 2)
        for copy in halo_copies(l, slot):
            copy.wait_recv()
        f = field[l]
        top = jnp.where(at_top, 0.0, halo_recv[slot, l, 0])
        bottom = jnp.where(at_bottom, 0.0, halo_recv[slot, l, 1])
        north = jnp.where(cell_row == 0, top, pltpu.roll(f, 1, 0))
        south = jnp.where(cell_row == 7, bottom, pltpu.roll(f, 7, 0))
        west = jnp.where(cell_col == 0, 0.0, pltpu.roll(f, 1, 1))
        east = jnp.where(cell_col == 2047, 0.0, pltpu.roll(f, 2047, 1))
        laplace = 4.0 * f - north - south - west - east

        if l == 0:
            @pl.when(sweep == 0)
            def _():
                for d in ORDER:
                    par_copy(d).wait_recv()

        weight = -beta[l]
        for c in range(16):
            lap[c % 2, pl.ds(c // 2, 8, stride=8), :] = weight * laplace[:, c * TILE:(c + 1) * TILE]
        is_odd = par_send[pl.ds(l, 1), :] > 0.5
        is_odd_from = {d: par[lax.rem(me + (NS - d), NS), pl.ds(l, 1), :] > 0.5 for d in ORDER}
        is_odd_to = {d: is_odd_from[NS - d] for d in ORDER}
        for q in range(PARTS):
            part = pl.ds(PART * q, PART)
            mine = own[PART * q:PART * (q + 1)]
            even_sum = lap[0, part, :] + jnp.where(is_odd, 0.0, mine)
            odd_sum = lap[1, part, :] + jnp.where(is_odd, mine, 0.0)
            for d in reversed(ORDER):
                b_copy(d, q).wait_recv()
                piece = b_recv[d, part, :]
                even_sum = even_sum + jnp.where(is_odd_from[d], 0.0, piece)
                odd_sum = odd_sum + jnp.where(is_odd_from[d], piece, 0.0)
            update = omega[l] * dot3(jnp.concatenate([even_sum, odd_sum], axis=0), m_hi[l], m_lo[l])
            even, odd_ = update[:PART], update[PART:]
            for d in ORDER:
                c_send[d, part, :] = jnp.where(is_odd_to[d], odd_, even)
                c_copy(d, q).start()
            upd[0, part, :] = even
            upd[1, part, :] = odd_
            halves[q][own_half, :] = jnp.where(is_odd, odd_, even)
        for c in range(16):
            field[l, :, c * TILE:(c + 1) * TILE] = (
                f[:, c * TILE:(c + 1) * TILE] + upd[c % 2, pl.ds(c // 2, 8, stride=8), :])
        for copy in halo_copies(l, slot):
            copy.wait_send()

        @pl.when(sweep < SWEEPS - 1)
        def _():
            halo_start(l, 1 - slot)

        @pl.when(sweep == SWEEPS - 1)
        def _():
            for d in ORDER:
                f_copy(l, d).start()

        for q in range(PARTS):
            for d in ORDER:
                b_copy(d, q).wait_send()
        none = jnp.zeros((8, TILE), jnp.float32)
        for q in range(PARTS):
            for d in ORDER:
                c_copy(d, q).wait_recv()
            columns = []
            for k in range(4):
                at = half[l] + k
                groups = [halves[q][pl.ds(SPAN * p + 8 + at, 8, stride=4), :] for p in range(8)]
                groups += [halves[q][pl.ds(4 + at, 8, stride=SPAN), :], none]
                columns.append(jnp.concatenate(groups, axis=0))
            change = dot3(jnp.concatenate(columns, axis=1), w_hi[l], w_lo[l])[:HALF]
            old = jnp.concatenate([win[pl.ds(LEAD + 16 * p + 8 * q, 8), :] for p in range(8)] + [none], axis=0)
            out[q] = old - jnp.where(line + (LEAD + 8 * q) >= start, change, 0.0)
            for n, dist in enumerate(FROM[l]):
                slot_copy(l, n, dist, q).start()
        for q in range(PARTS):
            for d in ORDER:
                c_copy(d, q).wait_send()

    def reframe(l):
        sources = FROM[l]
        least = min(sources[0], 0)
        base = -least * TD
        views = [(base, out)] + [(base + dist * TD, slots.at[SLOT0[l] + n]) for n, dist in enumerate(sources)]

        def place(at, view, q):
            for p in range(8):
                frame[pl.ds(LEAD + at + 16 * p + 8 * q, 8), :] = view[q, pl.ds(8 * p, 8), :]

        frame[pl.ds(0, LEAD), :] = jnp.zeros((LEAD, TILE), jnp.float32)
        for q in range(PARTS):
            place(*views[0], q)
        for q in range(PARTS):
            for n, dist in enumerate(sources):
                slot_copy(l, n, dist, q).wait_recv()
                place(*views[1 + n], q)
        for at, view in views:
            for q in range(PARTS):
                rows = pl.ds(LEAD - 1 + at + 8 * q, 8, stride=16)
                frame[rows, :] = frame[rows, :] + view[q, pl.ds(64, 8), :]
        moved = frame[pl.ds(base + lag[l] - lag[(l + 1) % LAYERS], WIN), :]
        for q in range(PARTS):
            for n, dist in enumerate(sources):
                slot_copy(l, n, dist, q).wait_send()
        win[...] = moved

    def turn(sweep, carry):
        for l in range(LAYERS):
            step(sweep, l)
            reframe(l)
        return carry

    lax.fori_loop(0, SWEEPS, turn, 0)
    residual_out[0] = win[pl.ds(LEAD, TD), :]
    store = pltpu.make_async_copy(field, layers_out.at[:, own_rows, :], local_sem.at[0])
    store.start()
    for d in ORDER:
        par_copy(d).wait_send()
    for l in range(LAYERS):
        for d in ORDER:
            f_copy(l, d).wait()
    store.wait()


def per_device(layers_init, residual_init, foot_shift, blocks, precond, omega, beta):
    vmem = pl.BlockSpec(memory_space=pltpu.VMEM)
    hbm = pl.BlockSpec(memory_space=pltpu.HBM)
    f32, bf16 = jnp.float32, jnp.bfloat16
    dma = pltpu.SemaphoreType.DMA
    return pl.pallas_call(
        kernel,
        out_shape=(
            jax.ShapeDtypeStruct(layers_init.shape, f32),
            jax.ShapeDtypeStruct(residual_init.shape, f32),
        ),
        in_specs=[hbm] * 7,
        out_specs=(hbm, vmem),
        scratch_shapes=[
            pltpu.SMEM((1, LAYERS), jnp.int32),
            pltpu.SMEM((LAYERS,), f32),
            pltpu.SMEM((LAYERS,), f32),
            pltpu.VMEM((LAYERS, 4, TILE, TILE), f32),
            pltpu.VMEM((LAYERS, TILE, TILE), f32),
            pltpu.VMEM((LAYERS, TILE, 4 * TILE), bf16),
            pltpu.VMEM((LAYERS, TILE, 4 * TILE), bf16),
            pltpu.VMEM((LAYERS, 4 * TILE, TILE), bf16),
            pltpu.VMEM((LAYERS, 4 * TILE, TILE), bf16),
            pltpu.VMEM((LAYERS, TILE, TILE), bf16),
            pltpu.VMEM((LAYERS, TILE, TILE), bf16),
            pltpu.VMEM((LAYERS, 8, 2048), f32),
            pltpu.VMEM((WIN, TILE), f32),
            pltpu.VMEM((LEAD + 7 * TD, TILE), f32),
            pltpu.VMEM((18, PARTS, HALF, TILE), f32),
            pltpu.VMEM((4 * WIN, TILE), f32),
            pltpu.VMEM((NS, PIECE, TILE), f32),
            pltpu.VMEM((NS, PIECE, TILE), f32),
            pltpu.VMEM((NS, PIECE, TILE), f32),
            pltpu.VMEM((8 * SPAN, TILE), f32),
            pltpu.VMEM((8 * SPAN, TILE), f32),
            pltpu.VMEM((PARTS, HALF, TILE), f32),
            pltpu.VMEM((8, TILE), f32),
            pltpu.VMEM((NS, 8, TILE), f32),
            pltpu.VMEM((2, PIECE, TILE), f32),
            pltpu.VMEM((2, PIECE, TILE), f32),
            pltpu.VMEM((LAYERS, 2, 1, 2048), f32),
            pltpu.VMEM((2, LAYERS, 2, 1, 2048), f32),
            dma((10,)), dma((PARTS, 18)), dma((PARTS, 18)), dma((PARTS, NS)), dma((PARTS, NS)), dma((PARTS, NS)), dma((PARTS, NS)),
            dma((NS,)), dma((NS,)),
            dma((LAYERS, 2)), dma((2, LAYERS, 2)), dma((LAYERS, NS)), dma((LAYERS, NS)),
        ],
        compiler_params=pltpu.CompilerParams(
            collective_id=0, has_side_effects=True, vmem_limit_bytes=63 * 2**20
        ),
    )(foot_shift, omega, beta, layers_init, residual_init, blocks, precond)


def solution(mesh):
    in_specs = (
        P(None, ("layer", "row"), None),
        P("sensor", ("layer", "row"), None),
        P("sensor", None),
        P("sensor", None, None, None, None),
        P(),
        P(),
        P(),
    )
    out_specs = (P(None, ("layer", "row"), None), P("sensor", ("layer", "row"), None))
    return jax.shard_map(
        per_device, mesh=mesh, in_specs=in_specs, out_specs=out_specs, check_vma=False
    )
```

```python
import functools

import jax
import jax.numpy as jnp
from jax import lax
from jax.experimental import pallas as pl
from jax.experimental.pallas import tpu as pltpu
from jax.sharding import PartitionSpec as P

MESH = pl.DeviceIdType.MESH
SWEEPS = 3
LAYERS = 4
NS = 8
NB = 32
ROWB = 4
TD = 128
TILE = 128
PIECE = 64
PARTS = 2
PART = PIECE // PARTS
SPAN = PART + 16
HALF = 72
WIN = 144
LEAD = 16
REACH = 3
ORDER = (4, 3, 5, 2, 6, 1, 7)
FROM = ((-3, -2, -1), (-3, -2, -1, 1, 2, 3), (-3, -2, -1, 1, 2, 3), (1, 2, 3))
SLOT0 = (0, 3, 9, 15)


def split(x):
    hi = x.astype(jnp.bfloat16)
    return hi, (x - hi.astype(jnp.float32)).astype(jnp.bfloat16)


def dot3(x, w_hi, w_lo):
    hi, lo = split(x)
    dot = functools.partial(jnp.dot, preferred_element_type=jnp.float32)
    return dot(hi, w_hi) + (dot(lo, w_hi) + dot(hi, w_lo))


def kernel(shift_in, omega_in, beta_in, layers_in, residual_in, blocks_in, precond_in,
           layers_out, residual_out,
           shift, omega, beta, raw, raw_m, wt_hi, wt_lo, w_hi, w_lo, m_hi, m_lo,
           field, win, frame, slots, flat, b_send, b_recv, c_send, halves_0, halves_1, out, par_send, par,
           lap, upd, halo_send, halo_recv,
           local_sem, slot_ssem, slot_rsem, b_ssem, b_rsem, c_ssem, c_rsem, p_ssem, p_rsem,
           h_ssem, h_rsem, f_ssem, f_rsem):
    lay, me, row = lax.axis_index("layer"), lax.axis_index("sensor"), lax.axis_index("row")
    block = lay * ROWB + row

    def at_block(dist):
        other = lax.rem(block + (dist + NB), NB)
        return (other // ROWB, me, lax.rem(other, ROWB))

    def at_sensor(dist):
        return (lay, lax.rem(me + dist, NS), row)

    first, last = me == 0, me == NS - 1
    up_block = lax.rem(block + NB - first.astype(jnp.int32), NB)
    down_block = lax.rem(block + last.astype(jnp.int32), NB)
    above = (up_block // ROWB, lax.rem(me + NS - 1, NS), lax.rem(up_block, ROWB))
    below = (down_block // ROWB, lax.rem(me + 1, NS), lax.rem(down_block, ROWB))

    barrier = pltpu.get_barrier_semaphore()
    partners = [at_sensor(d) for d in range(1, NS)]
    partners += [at_block(d) for d in (-3, -2, -1, 1, 2, 3)] + [above, below]
    for other in partners:
        pl.semaphore_signal(barrier, inc=1, device_id=other, device_id_type=MESH)

    own_rows = pl.ds(pl.multiple_of(me * 8, 8), 8)
    scalars = [
        pltpu.make_async_copy(shift_in, shift, local_sem.at[7]),
        pltpu.make_async_copy(omega_in, omega, local_sem.at[8]),
        pltpu.make_async_copy(beta_in, beta, local_sem.at[9]),
    ]
    for load in scalars:
        load.start()
    loads = [
        pltpu.make_async_copy(blocks_in.at[0, 0], raw.at[0], local_sem.at[0]),
        pltpu.make_async_copy(precond_in, raw_m, local_sem.at[1]),
        pltpu.make_async_copy(residual_in.at[0], win.at[pl.ds(LEAD, TD), :], local_sem.at[2]),
        pltpu.make_async_copy(layers_in.at[:, own_rows, :], field, local_sem.at[3]),
    ] + [pltpu.make_async_copy(blocks_in.at[0, l], raw.at[l], local_sem.at[3 + l]) for l in range(1, LAYERS)]
    for load in loads:
        load.start()
    frame[...] = jnp.zeros_like(frame)
    halves = (halves_0, halves_1)
    for buffer in halves:
        buffer[...] = jnp.zeros_like(buffer)
    win[pl.ds(0, LEAD), :] = jnp.zeros((LEAD, TILE), jnp.float32)
    for load in scalars:
        load.wait()
    odd = [lax.rem(shift[0, l], 2) for l in range(LAYERS)]
    half = [lax.rem(shift[0, l], 8) // 2 for l in range(LAYERS)]
    lag = [shift[0, l] // 8 for l in range(LAYERS)]
    for l in range(LAYERS):
        par_send[pl.ds(l, 1), :] = jnp.full((1, TILE), odd[l].astype(jnp.float32))
    par_send[pl.ds(LAYERS, 8 - LAYERS), :] = jnp.zeros((8 - LAYERS, TILE), jnp.float32)

    def prepare(l):
        m_hi[l], m_lo[l] = split(raw_m[l])
        for k in range(4):
            rows = pl.ds(k * TILE, TILE)
            block_k = raw[l, k]
            w_hi[l, rows, :], w_lo[l, rows, :] = split(block_k)
            wt_hi[l, :, k * TILE:(k + 1) * TILE], wt_lo[l, :, k * TILE:(k + 1) * TILE] = split(block_k.T)

    for load in loads[:2]:
        load.wait()
    prepare(0)
    for load in loads[2:4]:
        load.wait()
    for l in range(LAYERS):
        halo_send[l, 0] = field[l, pl.ds(0, 1), :]
        halo_send[l, 1] = field[l, pl.ds(7, 1), :]
    pl.semaphore_wait(barrier, len(partners))

    def par_copy(d):
        return pltpu.make_async_remote_copy(
            par_send, par.at[me], p_ssem.at[d], p_rsem.at[d], device_id=at_sensor(d), device_id_type=MESH)

    def halo_copies(l, slot):
        return [
            pltpu.make_async_remote_copy(
                halo_send.at[l, 0], halo_recv.at[slot, l, 1], h_ssem.at[l, 0], h_rsem.at[slot, l, 1],
                device_id=above, device_id_type=MESH),
            pltpu.make_async_remote_copy(
                halo_send.at[l, 1], halo_recv.at[slot, l, 0], h_ssem.at[l, 1], h_rsem.at[slot, l, 0],
                device_id=below, device_id_type=MESH),
        ]

    def halo_start(l, slot):
        halo_send[l, 0] = field[l, pl.ds(0, 1), :]
        halo_send[l, 1] = field[l, pl.ds(7, 1), :]
        for copy in halo_copies(l, slot):
            copy.start()

    for d in ORDER:
        par_copy(d).start()
    for l in range(LAYERS):
        for copy in halo_copies(l, 0):
            copy.start()

    def b_copy(d, q):
        part = pl.ds(PART * q, PART)
        return pltpu.make_async_remote_copy(
            b_send.at[d, part, :], b_recv.at[d, part, :], b_ssem.at[q, d], b_rsem.at[q, d], device_id=at_sensor(d), device_id_type=MESH)

    own_half = pl.ds(pl.multiple_of(SPAN * me + 8, 8), PART)

    def c_copy(d, q):
        return pltpu.make_async_remote_copy(
            c_send.at[d, pl.ds(PART * q, PART), :], halves[q].at[own_half, :], c_ssem.at[q, d], c_rsem.at[q, d],
            device_id=at_sensor(d), device_id_type=MESH)

    def f_copy(l, d):
        return pltpu.make_async_remote_copy(
            field.at[l], layers_out.at[l, pl.ds(pl.multiple_of(me * 8, 8), 8), :], f_ssem.at[l, d], f_rsem.at[l, d],
            device_id=at_sensor(d), device_id_type=MESH)

    def slot_copy(l, n, dist, q):
        n += SLOT0[l]
        return pltpu.make_async_remote_copy(
            out.at[q], slots.at[n, q], slot_ssem.at[q, n], slot_rsem.at[q, n],
            device_id=at_block(-dist), device_id_type=MESH)

    index = lax.broadcasted_iota(jnp.int32, (WIN, TILE), 0)
    line = lax.broadcasted_iota(jnp.int32, (HALF, TILE), 0)
    line = jnp.where(line < 64, 2 * line - (line & 7), 16 * line - 1025)
    cell_row = lax.broadcasted_iota(jnp.int32, (8, 2048), 0)
    cell_col = lax.broadcasted_iota(jnp.int32, (8, 2048), 1)
    at_top = jnp.logical_and(block == 0, first)
    at_bottom = jnp.logical_and(block == NB - 1, last)

    def sent(l):
        for q in range(PARTS):
            for n, dist in enumerate(FROM[l]):
                slot_copy(l, n, dist, q).wait_send()

    def step(sweep, l):
        start = LEAD + lag[l] - TD * block
        inside = index >= start
        products = dot3(jnp.where(inside, win[...], 0.0), wt_hi[l], wt_lo[l])
        for k in range(4):
            flat[pl.ds(k, WIN, stride=4), :] = products[:, k * TILE:(k + 1) * TILE]
        for q in range(PARTS):
            for d in ORDER:
                to = lax.rem(me + d, NS)
                b_send[d, pl.ds(PART * q, PART), :] = flat[pl.ds(64 + PIECE * to + PART * q - half[l], PART), :]
                b_copy(d, q).start()
        own = flat[pl.ds(64 + PIECE * me - half[l], PIECE), :]
        if l == 0:
            @pl.when(sweep == 0)
            def _():
                for other in range(1, LAYERS):
                    loads[3 + other].wait()
                    prepare(other)
        slot = lax.rem(sweep, 2)
        for copy in halo_copies(l, slot):
            copy.wait_recv()
        f = field[l]
        top = jnp.where(at_top, 0.0, halo_recv[slot, l, 0])
        bottom = jnp.where(at_bottom, 0.0, halo_recv[slot, l, 1])
        north = jnp.where(cell_row == 0, top, pltpu.roll(f, 1, 0))
        south = jnp.where(cell_row == 7, bottom, pltpu.roll(f, 7, 0))
        west = jnp.where(cell_col == 0, 0.0, pltpu.roll(f, 1, 1))
        east = jnp.where(cell_col == 2047, 0.0, pltpu.roll(f, 2047, 1))
        laplace = 4.0 * f - north - south - west - east

        if l == 0:
            @pl.when(sweep == 0)
            def _():
                for d in ORDER:
                    par_copy(d).wait_recv()

        weight = -beta[l]
        for c in range(16):
            lap[c % 2, pl.ds(c // 2, 8, stride=8), :] = weight * laplace[:, c * TILE:(c + 1) * TILE]
        is_odd = par_send[pl.ds(l, 1), :] > 0.5
        is_odd_from = {d: par[lax.rem(me + (NS - d), NS), pl.ds(l, 1), :] > 0.5 for d in ORDER}
        is_odd_to = {d: is_odd_from[NS - d] for d in ORDER}
        for q in range(PARTS):
            part = pl.ds(PART * q, PART)
            mine = own[PART * q:PART * (q + 1)]
            even_sum = lap[0, part, :] + jnp.where(is_odd, 0.0, mine)
            odd_sum = lap[1, part, :] + jnp.where(is_odd, mine, 0.0)
            for d in reversed(ORDER):
                b_copy(d, q).wait_recv()
                piece = b_recv[d, part, :]
                even_sum = even_sum + jnp.where(is_odd_from[d], 0.0, piece)
                odd_sum = odd_sum + jnp.where(is_odd_from[d], piece, 0.0)
            update = omega[l] * dot3(jnp.concatenate([even_sum, odd_sum], axis=0), m_hi[l], m_lo[l])
            even, odd_ = update[:PART], update[PART:]
            for d in ORDER:
                c_send[d, part, :] = jnp.where(is_odd_to[d], odd_, even)
                c_copy(d, q).start()
            upd[0, part, :] = even
            upd[1, part, :] = odd_
            halves[q][own_half, :] = jnp.where(is_odd, odd_, even)
        for c in range(16):
            field[l, :, c * TILE:(c + 1) * TILE] = (
                f[:, c * TILE:(c + 1) * TILE] + upd[c % 2, pl.ds(c // 2, 8, stride=8), :])
        for copy in halo_copies(l, slot):
            copy.wait_send()

        @pl.when(sweep < SWEEPS - 1)
        def _():
            halo_start(l, 1 - slot)

        @pl.when(sweep == SWEEPS - 1)
        def _():
            for d in ORDER:
                f_copy(l, d).start()

        for q in range(PARTS):
            for d in ORDER:
                b_copy(d, q).wait_send()
        if l == 0:
            @pl.when(sweep > 0)
            def _():
                sent(LAYERS - 1)
        else:
            sent(l - 1)
        none = jnp.zeros((8, TILE), jnp.float32)
        for q in range(PARTS):
            for d in ORDER:
                c_copy(d, q).wait_recv()
            columns = []
            for k in range(4):
                at = half[l] + k
                groups = [halves[q][pl.ds(SPAN * p + 8 + at, 8, stride=4), :] for p in range(8)]
                groups += [halves[q][pl.ds(4 + at, 8, stride=SPAN), :], none]
                columns.append(jnp.concatenate(groups, axis=0))
            change = dot3(jnp.concatenate(columns, axis=1), w_hi[l], w_lo[l])[:HALF]
            old = jnp.concatenate([win[pl.ds(LEAD + 16 * p + 8 * q, 8), :] for p in range(8)] + [none], axis=0)
            out[q] = old - jnp.where(line + (LEAD + 8 * q) >= start, change, 0.0)
            for n, dist in enumerate(FROM[l]):
                slot_copy(l, n, dist, q).start()
        for q in range(PARTS):
            for d in ORDER:
                c_copy(d, q).wait_send()

    def reframe(l):
        sources = FROM[l]
        least = min(sources[0], 0)
        base = -least * TD
        views = [(base, out)] + [(base + dist * TD, slots.at[SLOT0[l] + n]) for n, dist in enumerate(sources)]

        def place(at, view, q):
            for p in range(8):
                frame[pl.ds(LEAD + at + 16 * p + 8 * q, 8), :] = view[q, pl.ds(8 * p, 8), :]

        frame[pl.ds(0, LEAD), :] = jnp.zeros((LEAD, TILE), jnp.float32)
        def correct(at, view, q):
            rows = pl.ds(LEAD - 1 + at + 8 * q, 8, stride=16)
            frame[rows, :] = frame[rows, :] + view[q, pl.ds(64, 8), :]

        for q in range(PARTS):
            place(*views[0], q)
        correct(*views[0], 1)
        for q in range(PARTS):
            for n, dist in enumerate(sources):
                slot_copy(l, n, dist, q).wait_recv()
                place(*views[1 + n], q)
                if q:
                    correct(*views[1 + n], 1)
                    correct(*views[1 + n], 0)
        correct(*views[0], 0)
        moved = frame[pl.ds(base + lag[l] - lag[(l + 1) % LAYERS], WIN), :]
        win[...] = moved

    def turn(sweep, carry):
        for l in range(LAYERS):
            step(sweep, l)
            reframe(l)
        return carry

    lax.fori_loop(0, SWEEPS, turn, 0)
    sent(LAYERS - 1)
    residual_out[0] = win[pl.ds(LEAD, TD), :]
    store = pltpu.make_async_copy(field, layers_out.at[:, own_rows, :], local_sem.at[0])
    store.start()
    for d in ORDER:
        par_copy(d).wait_send()
    for l in range(LAYERS):
        for d in ORDER:
            f_copy(l, d).wait()
    store.wait()


def per_device(layers_init, residual_init, foot_shift, blocks, precond, omega, beta):
    vmem = pl.BlockSpec(memory_space=pltpu.VMEM)
    hbm = pl.BlockSpec(memory_space=pltpu.HBM)
    f32, bf16 = jnp.float32, jnp.bfloat16
    dma = pltpu.SemaphoreType.DMA
    return pl.pallas_call(
        kernel,
        out_shape=(
            jax.ShapeDtypeStruct(layers_init.shape, f32),
            jax.ShapeDtypeStruct(residual_init.shape, f32),
        ),
        in_specs=[hbm] * 7,
        out_specs=(hbm, vmem),
        scratch_shapes=[
            pltpu.SMEM((1, LAYERS), jnp.int32),
            pltpu.SMEM((LAYERS,), f32),
            pltpu.SMEM((LAYERS,), f32),
            pltpu.VMEM((LAYERS, 4, TILE, TILE), f32),
            pltpu.VMEM((LAYERS, TILE, TILE), f32),
            pltpu.VMEM((LAYERS, TILE, 4 * TILE), bf16),
            pltpu.VMEM((LAYERS, TILE, 4 * TILE), bf16),
            pltpu.VMEM((LAYERS, 4 * TILE, TILE), bf16),
            pltpu.VMEM((LAYERS, 4 * TILE, TILE), bf16),
            pltpu.VMEM((LAYERS, TILE, TILE), bf16),
            pltpu.VMEM((LAYERS, TILE, TILE), bf16),
            pltpu.VMEM((LAYERS, 8, 2048), f32),
            pltpu.VMEM((WIN, TILE), f32),
            pltpu.VMEM((LEAD + 7 * TD, TILE), f32),
            pltpu.VMEM((18, PARTS, HALF, TILE), f32),
            pltpu.VMEM((4 * WIN, TILE), f32),
            pltpu.VMEM((NS, PIECE, TILE), f32),
            pltpu.VMEM((NS, PIECE, TILE), f32),
            pltpu.VMEM((NS, PIECE, TILE), f32),
            pltpu.VMEM((8 * SPAN, TILE), f32),
            pltpu.VMEM((8 * SPAN, TILE), f32),
            pltpu.VMEM((PARTS, HALF, TILE), f32),
            pltpu.VMEM((8, TILE), f32),
            pltpu.VMEM((NS, 8, TILE), f32),
            pltpu.VMEM((2, PIECE, TILE), f32),
            pltpu.VMEM((2, PIECE, TILE), f32),
            pltpu.VMEM((LAYERS, 2, 1, 2048), f32),
            pltpu.VMEM((2, LAYERS, 2, 1, 2048), f32),
            dma((10,)), dma((PARTS, 18)), dma((PARTS, 18)), dma((PARTS, NS)), dma((PARTS, NS)), dma((PARTS, NS)), dma((PARTS, NS)),
            dma((NS,)), dma((NS,)),
            dma((LAYERS, 2)), dma((2, LAYERS, 2)), dma((LAYERS, NS)), dma((LAYERS, NS)),
        ],
        compiler_params=pltpu.CompilerParams(
            collective_id=0, has_side_effects=True, vmem_limit_bytes=63 * 2**20
        ),
    )(foot_shift, omega, beta, layers_init, residual_init, blocks, precond)


def solution(mesh):
    in_specs = (
        P(None, ("layer", "row"), None),
        P("sensor", ("layer", "row"), None),
        P("sensor", None),
        P("sensor", None, None, None, None),
        P(),
        P(),
        P(),
    )
    out_specs = (P(None, ("layer", "row"), None), P("sensor", ("layer", "row"), None))
    return jax.shard_map(
        per_device, mesh=mesh, in_specs=in_specs, out_specs=out_specs, check_vma=False
    )
```

```python
import functools

import jax
import jax.numpy as jnp
from jax import lax
from jax.experimental import pallas as pl
from jax.experimental.pallas import tpu as pltpu
from jax.sharding import PartitionSpec as P

MESH = pl.DeviceIdType.MESH
SWEEPS = 3
LAYERS = 4
NS = 8
NB = 32
ROWB = 4
TD = 128
TILE = 128
PIECE = 64
PARTS = 2
PART = PIECE // PARTS
SPAN = PART + 16
HALF = 72
WIN = 144
LEAD = 16
REACH = 3
ORDER = (4, 3, 5, 2, 6, 1, 7)
FROM = ((-3, -2, -1), (-3, -2, -1, 1, 2, 3), (-3, -2, -1, 1, 2, 3), (1, 2, 3))
SLOT0 = (0, 3, 9, 15)


def split(x):
    hi = x.astype(jnp.bfloat16)
    return hi, (x - hi.astype(jnp.float32)).astype(jnp.bfloat16)


def dot3(x, w_hi, w_lo):
    hi, lo = split(x)
    dot = functools.partial(jnp.dot, preferred_element_type=jnp.float32)
    return dot(hi, w_hi) + (dot(lo, w_hi) + dot(hi, w_lo))


def kernel(shift_in, omega_in, beta_in, layers_in, residual_in, blocks_in, precond_in,
           layers_out, residual_out,
           shift, omega, beta, raw, raw_m, wt_hi, wt_lo, w_hi, w_lo, m_hi, m_lo,
           field, win, frame, slots, flat, b_send, b_recv, c_send, halves_0, halves_1, out, par_send, par,
           lap, upd, halo_send, halo_recv,
           local_sem, slot_ssem, slot_rsem, b_ssem, b_rsem, c_ssem, c_rsem, p_ssem, p_rsem,
           h_ssem, h_rsem, f_ssem, f_rsem):
    lay, me, row = lax.axis_index("layer"), lax.axis_index("sensor"), lax.axis_index("row")
    block = lay * ROWB + row

    def at_block(dist):
        other = lax.rem(block + (dist + NB), NB)
        return (other // ROWB, me, lax.rem(other, ROWB))

    def at_sensor(dist):
        return (lay, lax.rem(me + dist, NS), row)

    first, last = me == 0, me == NS - 1
    up_block = lax.rem(block + NB - first.astype(jnp.int32), NB)
    down_block = lax.rem(block + last.astype(jnp.int32), NB)
    above = (up_block // ROWB, lax.rem(me + NS - 1, NS), lax.rem(up_block, ROWB))
    below = (down_block // ROWB, lax.rem(me + 1, NS), lax.rem(down_block, ROWB))

    barrier = pltpu.get_barrier_semaphore()
    partners = [at_sensor(d) for d in range(1, NS)]
    partners += [at_block(d) for d in (-3, -2, -1, 1, 2, 3)] + [above, below]
    for other in partners:
        pl.semaphore_signal(barrier, inc=1, device_id=other, device_id_type=MESH)

    own_rows = pl.ds(pl.multiple_of(me * 8, 8), 8)
    scalars = [
        pltpu.make_async_copy(shift_in, shift, local_sem.at[7]),
        pltpu.make_async_copy(omega_in, omega, local_sem.at[8]),
        pltpu.make_async_copy(beta_in, beta, local_sem.at[9]),
    ]
    for load in scalars:
        load.start()
    loads = [
        pltpu.make_async_copy(blocks_in.at[0, 0], raw.at[0], local_sem.at[0]),
        pltpu.make_async_copy(precond_in, raw_m, local_sem.at[1]),
        pltpu.make_async_copy(residual_in.at[0], win.at[pl.ds(LEAD, TD), :], local_sem.at[2]),
        pltpu.make_async_copy(layers_in.at[:, own_rows, :], field, local_sem.at[3]),
    ] + [pltpu.make_async_copy(blocks_in.at[0, l], raw.at[l], local_sem.at[3 + l]) for l in range(1, LAYERS)]
    for load in loads:
        load.start()
    frame[...] = jnp.zeros_like(frame)
    halves = (halves_0, halves_1)
    for buffer in halves:
        buffer[...] = jnp.zeros_like(buffer)
    win[pl.ds(0, LEAD), :] = jnp.zeros((LEAD, TILE), jnp.float32)
    for load in scalars:
        load.wait()
    odd = [lax.rem(shift[0, l], 2) for l in range(LAYERS)]
    half = [lax.rem(shift[0, l], 8) // 2 for l in range(LAYERS)]
    lag = [shift[0, l] // 8 for l in range(LAYERS)]
    for l in range(LAYERS):
        par_send[pl.ds(l, 1), :] = jnp.full((1, TILE), odd[l].astype(jnp.float32))
    par_send[pl.ds(LAYERS, 8 - LAYERS), :] = jnp.zeros((8 - LAYERS, TILE), jnp.float32)

    def prepare(l):
        m_hi[l], m_lo[l] = split(raw_m[l])
        for k in range(4):
            rows = pl.ds(k * TILE, TILE)
            block_k = raw[l, k]
            w_hi[l, rows, :], w_lo[l, rows, :] = split(block_k)
            wt_hi[l, :, k * TILE:(k + 1) * TILE], wt_lo[l, :, k * TILE:(k + 1) * TILE] = split(block_k.T)

    for load in loads[:2]:
        load.wait()
    prepare(0)
    for load in loads[2:4]:
        load.wait()
    for l in range(LAYERS):
        halo_send[l, 0] = field[l, pl.ds(0, 1), :]
        halo_send[l, 1] = field[l, pl.ds(7, 1), :]
    pl.semaphore_wait(barrier, len(partners))

    def par_copy(d):
        return pltpu.make_async_remote_copy(
            par_send, par.at[me], p_ssem.at[d], p_rsem.at[d], device_id=at_sensor(d), device_id_type=MESH)

    def halo_copies(l, slot):
        return [
            pltpu.make_async_remote_copy(
                halo_send.at[l, 0], halo_recv.at[slot, l, 1], h_ssem.at[l, 0], h_rsem.at[slot, l, 1],
                device_id=above, device_id_type=MESH),
            pltpu.make_async_remote_copy(
                halo_send.at[l, 1], halo_recv.at[slot, l, 0], h_ssem.at[l, 1], h_rsem.at[slot, l, 0],
                device_id=below, device_id_type=MESH),
        ]

    def halo_start(l, slot):
        halo_send[l, 0] = field[l, pl.ds(0, 1), :]
        halo_send[l, 1] = field[l, pl.ds(7, 1), :]
        for copy in halo_copies(l, slot):
            copy.start()

    for d in ORDER:
        par_copy(d).start()
    for l in range(LAYERS):
        for copy in halo_copies(l, 0):
            copy.start()

    def b_copy(d, q):
        part = pl.ds(PART * q, PART)
        return pltpu.make_async_remote_copy(
            b_send.at[d, part, :], b_recv.at[d, part, :], b_ssem.at[q, d], b_rsem.at[q, d], device_id=at_sensor(d), device_id_type=MESH)

    own_half = pl.ds(pl.multiple_of(SPAN * me + 8, 8), PART)

    def c_copy(d, q):
        return pltpu.make_async_remote_copy(
            c_send.at[d, pl.ds(PART * q, PART), :], halves[q].at[own_half, :], c_ssem.at[q, d], c_rsem.at[q, d],
            device_id=at_sensor(d), device_id_type=MESH)

    def f_copy(l, d):
        return pltpu.make_async_remote_copy(
            field.at[l], layers_out.at[l, pl.ds(pl.multiple_of(me * 8, 8), 8), :], f_ssem.at[l, d], f_rsem.at[l, d],
            device_id=at_sensor(d), device_id_type=MESH)

    def slot_copy(l, n, dist, q):
        n += SLOT0[l]
        return pltpu.make_async_remote_copy(
            out.at[q], slots.at[n, q], slot_ssem.at[q, n], slot_rsem.at[q, n],
            device_id=at_block(-dist), device_id_type=MESH)

    index = lax.broadcasted_iota(jnp.int32, (WIN, TILE), 0)
    line = lax.broadcasted_iota(jnp.int32, (HALF, TILE), 0)
    line = jnp.where(line < 64, 2 * line - (line & 7), 16 * line - 1025)
    cell_row = lax.broadcasted_iota(jnp.int32, (8, 2048), 0)
    cell_col = lax.broadcasted_iota(jnp.int32, (8, 2048), 1)
    at_top = jnp.logical_and(block == 0, first)
    at_bottom = jnp.logical_and(block == NB - 1, last)

    def step(sweep, l):
        start = LEAD + lag[l] - TD * block
        inside = index >= start
        products = dot3(jnp.where(inside, win[...], 0.0), wt_hi[l], wt_lo[l])
        for k in range(4):
            flat[pl.ds(k, WIN, stride=4), :] = products[:, k * TILE:(k + 1) * TILE]
        for q in range(PARTS):
            for d in ORDER:
                to = lax.rem(me + d, NS)
                b_send[d, pl.ds(PART * q, PART), :] = flat[pl.ds(64 + PIECE * to + PART * q - half[l], PART), :]
                b_copy(d, q).start()
        own = flat[pl.ds(64 + PIECE * me - half[l], PIECE), :]
        if l == 0:
            @pl.when(sweep == 0)
            def _():
                for other in range(1, LAYERS):
                    loads[3 + other].wait()
                    prepare(other)
        slot = lax.rem(sweep, 2)
        for copy in halo_copies(l, slot):
            copy.wait_recv()
        f = field[l]
        top = jnp.where(at_top, 0.0, halo_recv[slot, l, 0])
        bottom = jnp.where(at_bottom, 0.0, halo_recv[slot, l, 1])
        north = jnp.where(cell_row == 0, top, pltpu.roll(f, 1, 0))
        south = jnp.where(cell_row == 7, bottom, pltpu.roll(f, 7, 0))
        west = jnp.where(cell_col == 0, 0.0, pltpu.roll(f, 1, 1))
        east = jnp.where(cell_col == 2047, 0.0, pltpu.roll(f, 2047, 1))
        laplace = 4.0 * f - north - south - west - east

        if l == 0:
            @pl.when(sweep == 0)
            def _():
                for d in ORDER:
                    par_copy(d).wait_recv()

        weight = -beta[l]
        for c in range(16):
            lap[c % 2, pl.ds(c // 2, 8, stride=8), :] = weight * laplace[:, c * TILE:(c + 1) * TILE]
        is_odd = par_send[pl.ds(l, 1), :] > 0.5
        is_odd_from = {d: par[lax.rem(me + (NS - d), NS), pl.ds(l, 1), :] > 0.5 for d in ORDER}
        is_odd_to = {d: is_odd_from[NS - d] for d in ORDER}
        for q in range(PARTS):
            part = pl.ds(PART * q, PART)
            mine = own[PART * q:PART * (q + 1)]
            even_sum = lap[0, part, :] + jnp.where(is_odd, 0.0, mine)
            odd_sum = lap[1, part, :] + jnp.where(is_odd, mine, 0.0)
            for d in reversed(ORDER):
                b_copy(d, q).wait_recv()
                piece = b_recv[d, part, :]
                even_sum = even_sum + jnp.where(is_odd_from[d], 0.0, piece)
                odd_sum = odd_sum + jnp.where(is_odd_from[d], piece, 0.0)
            update = omega[l] * dot3(jnp.concatenate([even_sum, odd_sum], axis=0), m_hi[l], m_lo[l])
            even, odd_ = update[:PART], update[PART:]
            for d in ORDER:
                c_send[d, part, :] = jnp.where(is_odd_to[d], odd_, even)
                c_copy(d, q).start()
            upd[0, part, :] = even
            upd[1, part, :] = odd_
            halves[q][own_half, :] = jnp.where(is_odd, odd_, even)
        for c in range(16):
            field[l, :, c * TILE:(c + 1) * TILE] = (
                f[:, c * TILE:(c + 1) * TILE] + upd[c % 2, pl.ds(c // 2, 8, stride=8), :])
        for copy in halo_copies(l, slot):
            copy.wait_send()

        @pl.when(sweep < SWEEPS - 1)
        def _():
            halo_start(l, 1 - slot)

        def share():
            @pl.when(sweep == SWEEPS - 1)
            def _():
                for d in ORDER:
                    f_copy(l, d).start()

        if l == LAYERS - 1:
            share()

        for q in range(PARTS):
            for d in ORDER:
                b_copy(d, q).wait_send()
        none = jnp.zeros((8, TILE), jnp.float32)
        for q in range(PARTS):
            for d in ORDER:
                c_copy(d, q).wait_recv()
            columns = []
            for k in range(4):
                at = half[l] + k
                groups = [halves[q][pl.ds(SPAN * p + 8 + at, 8, stride=4), :] for p in range(8)]
                groups += [halves[q][pl.ds(4 + at, 8, stride=SPAN), :], none]
                columns.append(jnp.concatenate(groups, axis=0))
            change = dot3(jnp.concatenate(columns, axis=1), w_hi[l], w_lo[l])[:HALF]
            old = jnp.concatenate([win[pl.ds(LEAD + 16 * p + 8 * q, 8), :] for p in range(8)] + [none], axis=0)
            out[q] = old - jnp.where(line + (LEAD + 8 * q) >= start, change, 0.0)
            for n, dist in enumerate(FROM[l]):
                slot_copy(l, n, dist, q).start()
            if q == 0 and l < LAYERS - 1:
                share()
        for q in range(PARTS):
            for d in ORDER:
                c_copy(d, q).wait_send()

    def reframe(l):
        sources = FROM[l]
        least = min(sources[0], 0)
        base = -least * TD
        views = [(base, out)] + [(base + dist * TD, slots.at[SLOT0[l] + n]) for n, dist in enumerate(sources)]

        def place(at, view, q):
            for p in range(8):
                frame[pl.ds(LEAD + at + 16 * p + 8 * q, 8), :] = view[q, pl.ds(8 * p, 8), :]

        frame[pl.ds(0, LEAD), :] = jnp.zeros((LEAD, TILE), jnp.float32)
        for q in range(PARTS):
            place(*views[0], q)
        for q in range(PARTS):
            for n, dist in enumerate(sources):
                slot_copy(l, n, dist, q).wait_recv()
                place(*views[1 + n], q)
        for at, view in views:
            for q in range(PARTS):
                rows = pl.ds(LEAD - 1 + at + 8 * q, 8, stride=16)
                frame[rows, :] = frame[rows, :] + view[q, pl.ds(64, 8), :]
        moved = frame[pl.ds(base + lag[l] - lag[(l + 1) % LAYERS], WIN), :]
        for q in range(PARTS):
            for n, dist in enumerate(sources):
                slot_copy(l, n, dist, q).wait_send()
        win[...] = moved

    def turn(sweep, carry):
        for l in range(LAYERS):
            step(sweep, l)
            reframe(l)
        return carry

    lax.fori_loop(0, SWEEPS, turn, 0)
    residual_out[0] = win[pl.ds(LEAD, TD), :]
    store = pltpu.make_async_copy(field, layers_out.at[:, own_rows, :], local_sem.at[0])
    store.start()
    for d in ORDER:
        par_copy(d).wait_send()
    for l in range(LAYERS):
        for d in ORDER:
            f_copy(l, d).wait()
    store.wait()


def per_device(layers_init, residual_init, foot_shift, blocks, precond, omega, beta):
    vmem = pl.BlockSpec(memory_space=pltpu.VMEM)
    hbm = pl.BlockSpec(memory_space=pltpu.HBM)
    f32, bf16 = jnp.float32, jnp.bfloat16
    dma = pltpu.SemaphoreType.DMA
    return pl.pallas_call(
        kernel,
        out_shape=(
            jax.ShapeDtypeStruct(layers_init.shape, f32),
            jax.ShapeDtypeStruct(residual_init.shape, f32),
        ),
        in_specs=[hbm] * 7,
        out_specs=(hbm, vmem),
        scratch_shapes=[
            pltpu.SMEM((1, LAYERS), jnp.int32),
            pltpu.SMEM((LAYERS,), f32),
            pltpu.SMEM((LAYERS,), f32),
            pltpu.VMEM((LAYERS, 4, TILE, TILE), f32),
            pltpu.VMEM((LAYERS, TILE, TILE), f32),
            pltpu.VMEM((LAYERS, TILE, 4 * TILE), bf16),
            pltpu.VMEM((LAYERS, TILE, 4 * TILE), bf16),
            pltpu.VMEM((LAYERS, 4 * TILE, TILE), bf16),
            pltpu.VMEM((LAYERS, 4 * TILE, TILE), bf16),
            pltpu.VMEM((LAYERS, TILE, TILE), bf16),
            pltpu.VMEM((LAYERS, TILE, TILE), bf16),
            pltpu.VMEM((LAYERS, 8, 2048), f32),
            pltpu.VMEM((WIN, TILE), f32),
            pltpu.VMEM((LEAD + 7 * TD, TILE), f32),
            pltpu.VMEM((18, PARTS, HALF, TILE), f32),
            pltpu.VMEM((4 * WIN, TILE), f32),
            pltpu.VMEM((NS, PIECE, TILE), f32),
            pltpu.VMEM((NS, PIECE, TILE), f32),
            pltpu.VMEM((NS, PIECE, TILE), f32),
            pltpu.VMEM((8 * SPAN, TILE), f32),
            pltpu.VMEM((8 * SPAN, TILE), f32),
            pltpu.VMEM((PARTS, HALF, TILE), f32),
            pltpu.VMEM((8, TILE), f32),
            pltpu.VMEM((NS, 8, TILE), f32),
            pltpu.VMEM((2, PIECE, TILE), f32),
            pltpu.VMEM((2, PIECE, TILE), f32),
            pltpu.VMEM((LAYERS, 2, 1, 2048), f32),
            pltpu.VMEM((2, LAYERS, 2, 1, 2048), f32),
            dma((10,)), dma((PARTS, 18)), dma((PARTS, 18)), dma((PARTS, NS)), dma((PARTS, NS)), dma((PARTS, NS)), dma((PARTS, NS)),
            dma((NS,)), dma((NS,)),
            dma((LAYERS, 2)), dma((2, LAYERS, 2)), dma((LAYERS, NS)), dma((LAYERS, NS)),
        ],
        compiler_params=pltpu.CompilerParams(
            collective_id=0, has_side_effects=True, vmem_limit_bytes=63 * 2**20
        ),
    )(foot_shift, omega, beta, layers_init, residual_init, blocks, precond)


def solution(mesh):
    in_specs = (
        P(None, ("layer", "row"), None),
        P("sensor", ("layer", "row"), None),
        P("sensor", None),
        P("sensor", None, None, None, None),
        P(),
        P(),
        P(),
    )
    out_specs = (P(None, ("layer", "row"), None), P("sensor", ("layer", "row"), None))
    return jax.shard_map(
        per_device, mesh=mesh, in_specs=in_specs, out_specs=out_specs, check_vma=False
    )
```
